128 devices in a mesh: grp: 8 (over z_hi, y), tp: 16 (over z_lo, x, core).
Axes of the slice: x: 4, y: 4, z: 4 (z_hi: 2, z_lo: 2; z = z_hi * 2 + z_lo), core: 2. Of those that a mesh axis runs over, the one named last changes fastest.
Arguments:
- hidden: bfloat16 [12288, 8192], P(('grp', 'tp')), may hold values from -21 to 21
- boundaries: int32 [8, 128], P('grp'), may hold values from 0 to 1535, as said below
- wq_old: bfloat16 [8192, 4096], P(None, 'tp'), may hold values from -0.0625 to 0.0625
- wk_old: bfloat16 [8192, 512], P(None, 'tp'), may hold values from -0.0625 to 0.0625
- wv_old: bfloat16 [8192, 512], P(None, 'tp'), may hold values from -0.0625 to 0.0625
- wo_old: bfloat16 [4096, 8192], P('tp'), may hold values from -0.125 to 0.125
- weights: bfloat16 [8192, 4096], P(('grp', 'tp')), may hold values from -0.0625 to 0.0625
- grads: bfloat16 [8192, 4096], P(('grp', 'tp')), may hold values from -0.15625 to 0.15625
- moment: float32 [8192, 4096], P(('grp', 'tp')), may hold values from -0.015625 to 0.015625
- second: float32 [8192, 4096], P(('grp', 'tp')), may hold values from 1e-08 to 4e-07
Outputs:
- step_features: bfloat16 [1024, 8192], P('grp', 'tp')
- quantized: bfloat16 [8192, 4096], P(None, 'tp')
- scales: float32 [64, 32], P(None, 'tp')
The draws below stay inside these ranges and needn't reach their ends.
Inputs may be any that keep to these rules, and one draw needn't show every extreme that they name: `boundaries`: each row is strictly increasing and ends at 1535.
All inputs are finite; a program needn't handle non-finite values.
Results may differ from the reference program's by a relative error of at most 0.024.
The reference program's roundings to bfloat16 on the way count: a program that leaves them out, or rounds other values in their place, can miss the bound.
Values may be sent and summed in bfloat16 or wider, within the bound.
No kernel may reach another device: no remote copies, remote signals or barrier semaphores. Data moves between devices by JAX's collectives and lax.ppermute only.
A program may use at most 128 MiB of HBM per device.

```python
import math
import jax
import jax.numpy as jnp
from jax import lax

D = 8192
QH = 32
KVH = 4
HD = 128
BLOCK = 128
STEPS = 128
QW = 4096
SEQ = 1536
GROUPS = 8
N_TP = 16


def draw_hidden(key, part):
    key = jax.random.fold_in(key, 3)
    row_total = GROUPS * SEQ
    values = jnp.clip(jax.random.normal(key, (row_total, D), jnp.float32), -6.0, 6.0)
    return values.astype(jnp.bfloat16)


def draw_boundaries(key, part):
    key = jax.random.fold_in(key, 7)
    sub_keys = jax.random.split(key, GROUPS)

    def one_row(sub_key):
        order = jax.random.permutation(sub_key, SEQ - 1)
        chosen = jnp.sort(order[:STEPS - 1])
        return jnp.concatenate([chosen, jnp.array([SEQ - 1], jnp.int32)]).astype(jnp.int32)
    return jax.vmap(one_row)(sub_keys)


def spiked(values, rng, source, target, parts, factor):
    def block_of(dim):
        return (jnp.arange(values.shape[dim]) // (values.shape[dim] // parts)).reshape((-1,) + (1,) * (values.ndim - 1 - dim))

    one_side = jax.random.permutation(rng, parts)[block_of(target)]
    second = (block_of(target) + parts // 2) % parts
    return jnp.where((block_of(source) == one_side) | (block_of(source) == second), factor * values, values)


def levels(stream_key, extent, shards, low, largest):
    level = 1.0
    for position, shards_of in shards:
        heights = jax.random.uniform(jax.random.fold_in(jax.random.fold_in(stream_key, 6), position), (shards_of,), jnp.float32, low / len(shards), largest / len(shards))
        level = level * jnp.repeat(jnp.exp(heights), extent[position] // shards_of).reshape((-1,) + (1,) * (len(extent) - 1 - position))
    return level


def normal_values(key, shape, width, most, cuts=(), kind=jnp.bfloat16):
    drawn = width * jax.random.normal(key, shape, jnp.float32)
    if cuts:
        drawn = drawn * levels(key, shape, cuts, -0.22, 0.18)
    return jnp.clip(drawn, -most, most).astype(kind)


def heavy_noise(rng, dims, deviation, most, pieces, heavy, held_as=jnp.bfloat16):
    result = deviation * jax.random.normal(rng, dims, jnp.float32)
    if pieces:
        result = result * levels(rng, dims, pieces, -0.22, 0.18)
    return jnp.clip(spiked(result, jax.random.fold_in(rng, 3), *heavy), -most, most).astype(held_as)


def setup_inputs(seed: int = 0) -> dict:
    key_of = jax.random.split(jax.random.key(seed), 11)
    return {
        "hidden": draw_hidden(jax.random.fold_in(key_of[10], 71), 0),
        "boundaries": draw_boundaries(jax.random.fold_in(key_of[10], 71), 0),
        "wq_old": normal_values(key_of[2], (D, QW), D ** -0.5, 0.0625, ((1, 16),)),
        "wk_old": normal_values(key_of[3], (D, KVH * HD), D ** -0.5, 0.0625, ((1, 16),)),
        "wv_old": normal_values(key_of[4], (D, KVH * HD), D ** -0.5, 0.0625, ((1, 16),)),
        "wo_old": heavy_noise(key_of[5], (QW, D), QW ** -0.5, 0.125, ((0, 16),), (0, 1, 16, 2.0)),
        "weights": normal_values(key_of[6], (D, QW), D ** -0.5, 0.0625, ((0, 128),)),
        "grads": normal_values(key_of[7], (D, QW), 0.01, 0.15625, ((0, 128),)),
        "moment": normal_values(key_of[8], (D, QW), 0.001, 0.015625, ((0, 128),), jnp.float32),
        "second": jnp.clip(jnp.exp(math.log(4.0000000467443897e-07) - 3.6888795 * jax.random.uniform(key_of[9], (D, QW), jnp.float32) ** levels(key_of[9], (D, QW), ((0, 128),), -0.2, 0.2)), 9.99999993922529e-09, 4.0000000467443897e-07),
    }


def adam_fresh(weights, grads, moment, second):
    wfull = weights.astype(jnp.float32)
    gfull = grads.astype(jnp.float32)
    first_new = 0.9 * moment + 0.1 * gfull
    second_new = 0.999 * second + 0.001 * gfull * gfull
    corr_one = 1.0 - 0.9 ** 10
    corr_two = 1.0 - 0.999 ** 10
    update = first_new / corr_one / (jnp.sqrt(second_new / corr_two) + 1e-08)
    return (wfull - 0.02 * (update + 0.1 * wfull)).astype(jnp.bfloat16)

def block_quant(fresh):
    rows_all, cols_all = fresh.shape
    tiles = jnp.abs(fresh.astype(jnp.float32)).reshape(rows_all // BLOCK, BLOCK, cols_all // BLOCK, BLOCK)
    amax = lax.optimization_barrier(jnp.max(tiles, axis=(1, 3))) + 1e-06
    factor = 448.0 / amax
    spread = jnp.repeat(jnp.repeat(factor, BLOCK, axis=0), BLOCK, axis=1)
    quant = (fresh.astype(jnp.float32) * spread).astype(jnp.bfloat16)
    return (quant, amax / 448.0)

def score_group(inputs, wq_old, wk_old, wv_old, wo_old):
    seq_rows, bounds = inputs
    key_all = jnp.dot(seq_rows, wk_old, preferred_element_type=jnp.float32).astype(jnp.bfloat16)
    value_all = jnp.dot(seq_rows, wv_old, preferred_element_type=jnp.float32).astype(jnp.bfloat16)
    picked = seq_rows[bounds]
    queries = jnp.dot(picked, wq_old, preferred_element_type=jnp.float32).astype(jnp.bfloat16)
    ratio = QH // KVH
    query_f = queries.astype(jnp.float32).reshape(STEPS, KVH, ratio, HD)
    key_f = key_all.astype(jnp.float32).reshape(SEQ, KVH, HD)
    value_f = value_all.astype(jnp.float32).reshape(SEQ, KVH, HD)
    scores = jnp.einsum('sgrd,jgd->grsj', query_f, key_f) * (1.0 / jnp.sqrt(jnp.float32(HD)))
    visible = jnp.arange(SEQ)[None, :] <= bounds[:, None]
    scores = jnp.where(visible[None, None], scores, jnp.float32(-1e+30))
    row_peak = lax.optimization_barrier(jnp.max(scores, axis=-1, keepdims=True))
    expo = jnp.exp(scores - row_peak)
    probs = (expo / lax.optimization_barrier(jnp.sum(expo, axis=-1, keepdims=True))).astype(jnp.bfloat16)
    context = jnp.einsum('grsj,jgd->sgrd', probs.astype(jnp.float32), value_f).astype(jnp.bfloat16)
    context = context.reshape(STEPS, QH * HD)
    group_cols = QW // N_TP
    partial_value = jnp.einsum('snc,ncd->nsd', context.reshape(STEPS, N_TP, group_cols).astype(jnp.float32), wo_old.reshape(N_TP, group_cols, D).astype(jnp.float32))
    partial_value = partial_value.astype(jnp.bfloat16).astype(jnp.float32)
    return lax.optimization_barrier(jnp.sum(partial_value, axis=0)).astype(jnp.bfloat16)

def reference(hidden, boundaries, wq_old, wk_old, wv_old, wo_old, weights, grads, moment, second):
    per_seq = hidden.reshape(GROUPS, SEQ, D)
    outputs = lax.map(lambda item: score_group(item, wq_old, wk_old, wv_old, wo_old), (per_seq, boundaries))
    step_features = outputs.reshape(GROUPS * STEPS, D)
    fresh = adam_fresh(weights, grads, moment, second)
    quantized, scales = block_quant(fresh)
    return (step_features, quantized, scales)
```

```python
import jax
import jax.numpy as jnp
from jax import lax
from jax.sharding import PartitionSpec as P

KVH = 4
HD = 128
BLOCK = 128
AXES = ("grp", "tp")
NX = 4
F32 = jnp.float32
BF16 = jnp.bfloat16


def coords(i):
    return (i // 64, i // 16 % 4, i // 8 % 2, i // 2 % 4, i % 2)


def send(value, zh=0, y=0, zl=0, x=0, core=0, z=0):
    pairs = []
    for i in range(128):
        a, b, l, e, c = coords(i)
        zz = (2 * a + l + z) % 4
        a, l = zz // 2, zz % 2
        j = ((((a ^ zh) * 4 + (b + y) % 4) * 2 + (l ^ zl)) * 4 + (e + x) % 4) * 2 + (c ^ core)
        pairs.append((i, j))
    return lax.ppermute(value, AXES, pairs)


def put(buffer, block, *index):
    return lax.dynamic_update_slice(buffer, block, index)


def pick(value, index, axis):
    return lax.dynamic_index_in_dim(value, index, axis, keepdims=False)


def adam_fresh(weights, grads, moment, second):
    wfull = weights.astype(F32)
    gfull = grads.astype(F32)
    first_new = 0.9 * moment + 0.1 * gfull
    second_new = 0.999 * second + 0.001 * gfull * gfull
    corr_one = 1.0 - 0.9**10
    corr_two = 1.0 - 0.999**10
    update = first_new / corr_one / (jnp.sqrt(second_new / corr_two) + 1e-08)
    return (wfull - 0.02 * (update + 0.1 * wfull)).astype(BF16)


def block_quant(fresh):
    rows_all, cols_all = fresh.shape
    tiles = jnp.abs(fresh.astype(F32)).reshape(BLOCK, cols_all // BLOCK, BLOCK)
    amax = jnp.max(tiles, axis=(0, 2)) + 1e-06
    factor = 448.0 / amax
    spread = jnp.repeat(factor, BLOCK, axis=0)[None, :]
    quant = (fresh.astype(F32) * spread).astype(BF16)
    return (quant, amax / 448.0)


def on_device(hidden, boundaries, wq_old, wk_old, wv_old, wo_old, weights, grads, moment, second):
    gi = lax.axis_index("grp")
    ti = lax.axis_index("tp")
    zh, yy = gi // 4, gi % 4
    zl, xx, cc = ti // 8, ti // 2 % 4, ti % 2
    bounds = boundaries[0]
    tok, wide = hidden.shape
    steps = bounds.shape[0]
    at = lambda d: (xx + d) % 4
    zero = jnp.int32(0)

    zown = send(hidden, zl=1)
    oth = send(hidden, core=1)
    piece = jnp.concatenate([wk_old.T, wv_old.T], 0)
    half = piece.shape[0] // 2
    w_lo, w_hi = piece[:half], piece[half:]
    lo_p, hi_m = send(w_lo, x=1), send(w_hi, x=-1)
    hi_p, lo_m = send(w_hi, x=1), send(w_lo, x=-1)
    lo_pp, hi_mm = send(lo_p, x=1), send(hi_m, x=-1)

    fresh = adam_fresh(weights, grads, moment, second).reshape(64, 8, 2, 256)
    keep = pick(fresh, cc, 2).reshape(64, 2048)
    got = send(pick(fresh, 1 - cc, 2).reshape(64, 2048), core=1)
    full = jnp.where(cc == 0, jnp.concatenate([keep, got], 0), jnp.concatenate([got, keep], 0))
    quant, scale = block_quant(full)
    all_scales = lax.all_gather(scale.reshape(1, 16), AXES, axis=0, tiled=True)
    scales = pick(pick(all_scales.reshape(64, 2, 8, 2), cc, 1), zl * 4 + xx, 1)
    quant = quant.reshape(128, 2, 4, 256)
    qx = jnp.zeros((4, 128, 2, 256), BF16)
    qx = put(qx, pick(quant, xx, 2)[None], xx, zero, zero, zero)
    for d in (1, 3, 2):
        part = send(pick(quant, at(d), 2), x=d)
        qx = put(qx, part[None], at(-d), zero, zero, zero)
    qx = qx.reshape(512, 2, 256)
    z = 2 * zh + zl
    qz = jnp.zeros((4, 512, 256), BF16)
    qz = put(qz, pick(qx, zl, 1)[None], z, zero, zero)
    for d in (1, 3, 2):
        part = send(pick(qx, (zl + d) % 2, 1), z=d)
        qz = put(qz, part[None], (z - d) % 4, zero, zero)
    q_lo, q_hi = qz[:2].reshape(1, 1, 1024, 256), qz[2:].reshape(1, 1, 1024, 256)
    qlo_p, qhi_m = send(q_lo, y=1), send(q_hi, y=-1)
    qhi_p, qlo_m = send(q_hi, y=1), send(q_lo, y=-1)
    qlo_pp, qhi_mm = send(qlo_p, y=1), send(qhi_m, y=-1)
    quantized = jnp.zeros((2, 4, 1024, 256), BF16)
    for block, h, d in (
        (q_lo, 0, 0), (q_hi, 1, 0), (qlo_p, 0, -1), (qhi_p, 1, -1),
        (qlo_m, 0, 1), (qhi_m, 1, 1), (qlo_pp, 0, 2), (qhi_mm, 1, 2),
    ):
        quantized = put(quantized, block, jnp.int32(h), (yy + d) % 4, zero, zero)
    quantized = quantized.reshape(8192, 256)

    chip = jnp.where(cc == 0, jnp.concatenate([hidden, oth], 0), jnp.concatenate([oth, hidden], 0))
    places = (zl * 8 + xx * 2) * tok + lax.iota(jnp.int32, 2 * tok)
    picker = (bounds[:, None] == places[None, :]).astype(BF16)
    half_cols = lax.dynamic_slice(chip, (zero, cc * (wide // 2)), (2 * tok, wide // 2))
    mine = jnp.dot(picker, half_cols, preferred_element_type=F32).astype(BF16)
    mine = mine.reshape(steps, 4, 2, 512)
    acc = pick(mine, xx, 1)
    for d in (1, 3, 2):
        acc = acc + send(pick(mine, at(d), 1), x=d)
    acc = pick(acc, zl, 1) + send(pick(acc, 1 - zl, 1), zl=1)
    other = send(acc, zl=1)
    acc = jnp.where(zl == 0, jnp.concatenate([acc, other], 1), jnp.concatenate([other, acc], 1))
    rows_half = jnp.zeros((steps, 4096), BF16)
    rows_half = put(rows_half, acc, zero, xx * 1024)
    for d in (1, 3, 2):
        rows_half = put(rows_half, send(acc, x=d), zero, at(-d) * 1024)
    rows_other = send(rows_half, core=1)
    rows = jnp.where(
        cc == 0,
        jnp.concatenate([rows_half, rows_other], 1),
        jnp.concatenate([rows_other, rows_half], 1),
    )
    queries = jnp.dot(rows, wq_old, preferred_element_type=F32).astype(BF16)

    wall = jnp.zeros((4, 2 * half, wide), BF16)
    wall = put(wall, piece[None], xx, zero, zero)
    wall = put(wall, jnp.concatenate([lo_p, hi_p], 0)[None], at(-1), zero, zero)
    wall = put(wall, jnp.concatenate([lo_m, hi_m], 0)[None], at(1), zero, zero)
    wall = put(wall, jnp.concatenate([lo_pp, hi_mm], 0)[None], at(2), zero, zero)
    zoth = send(zown, core=1)
    zchip = jnp.where(cc == 0, jnp.concatenate([zown, zoth], 0), jnp.concatenate([zoth, zown], 0))
    wall = wall.reshape(8 * half, wide)
    tokens = jnp.concatenate([chip, zchip], 0)
    kv = lax.dot_general(wall, tokens, (((1,), (1,)), ((), ())), preferred_element_type=F32)
    kv = kv.astype(BF16).reshape(2, 2, 2 * half, 4 * tok)
    own_kv = pick(kv, xx // 2, 0)
    parts = [own_kv]
    for d in (1, 2, 3):
        parts.append(send(pick(kv, at(-d) // 2, 0), x=-d))
    kv_half = jnp.concatenate(parts, 2)
    kv_other = send(kv_half, core=1)
    both = jnp.where(cc == 0, jnp.stack([kv_half, kv_other]), jnp.stack([kv_other, kv_half]))
    both = both.reshape(2, 2, 2, 32, 16 * tok).transpose(2, 1, 0, 3, 4).reshape(2, HD, 16 * tok)
    key_head, value_head = both[0], both[1]

    slot = lax.iota(jnp.int32, 16 * tok)
    sx, sr, si = slot // (4 * tok), slot // (2 * tok) % 2, slot % (2 * tok)
    position = ((zl ^ sr) * 8 + (xx + sx) % 4 * 2) * tok + si

    head_count = queries.shape[1] // HD
    query_heads = queries.reshape(steps, head_count, HD)
    scores = jnp.einsum("shd,dj->hsj", query_heads, key_head, preferred_element_type=F32)
    scores = scores * (1.0 / jnp.sqrt(F32(HD)))
    visible = position[None, :] <= bounds[:, None]
    scores = jnp.where(visible[None], scores, F32(-1e30))
    row_peak = jnp.max(scores, axis=-1, keepdims=True)
    expo = jnp.exp(scores - row_peak)
    probs = (expo / jnp.sum(expo, axis=-1, keepdims=True)).astype(BF16)
    context = jnp.einsum("hsj,dj->shd", probs, value_head, preferred_element_type=F32)
    context = context.astype(BF16).reshape(steps, head_count * HD)

    wo_parts = wo_old.reshape(256, 8, 2, 512)
    wo_other = pick(wo_parts, 1 - cc, 2).reshape(256, 4096)
    wo_mine = pick(wo_parts, cc, 2).reshape(256, 4096)
    out_other = jnp.dot(context, wo_other, preferred_element_type=F32).astype(BF16)
    out_core = send(out_other, core=1)
    out_mine = jnp.dot(context, wo_mine, preferred_element_type=F32).astype(BF16)
    out = (out_mine.astype(F32) + out_core.astype(F32)).reshape(steps, 2, 4, 512)
    total = pick(out, xx, 2)
    out = out.astype(BF16)
    for d in (1, 3, 2):
        total = total + send(pick(out, at(d), 2), x=d).astype(F32)
    final = pick(total, zl, 1) + send(pick(total, 1 - zl, 1).astype(BF16), zl=1).astype(F32)
    step_features = final.astype(BF16)
    return (step_features, quantized, scales)


def solution(mesh):
    placed = (
        P(("grp", "tp"), None),
        P("grp", None),
        P(None, "tp"),
        P(None, "tp"),
        P(None, "tp"),
        P("tp", None),
        P(("grp", "tp"), None),
        P(("grp", "tp"), None),
        P(("grp", "tp"), None),
        P(("grp", "tp"), None),
    )
    return jax.shard_map(
        on_device,
        mesh=mesh,
        in_specs=placed,
        out_specs=(P("grp", "tp"), P(None, "tp"), P(None, "tp")),
        check_vma=False,
    )
```

```python
import jax
import jax.numpy as jnp
from jax import lax
from jax.experimental import pallas as pl
from jax.experimental.pallas import tpu as pltpu
from jax.sharding import PartitionSpec as P

HD = 128
BLOCK = 128
TOK = 96
WIDE = 8192
STEPS = 128
AXES = ("grp", "tp")
F32 = jnp.float32
BF16 = jnp.bfloat16


def coords(i):
    return (i // 64, i // 16 % 4, i // 8 % 2, i // 2 % 4, i % 2)


def send(value, y=0, zl=0, x=0, core=0):
    pairs = []
    for i in range(128):
        a, b, l, e, c = coords(i)
        j = (((a * 4 + (b + y) % 4) * 2 + (l ^ zl)) * 4 + (e + x) % 4) * 2 + (c ^ core)
        pairs.append((i, j))
    return lax.ppermute(value, AXES, pairs)


def place():
    ti = lax.axis_index("tp")
    return ti // 8, ti // 2 % 4, ti % 2


def nt_dot(a, b):
    return lax.dot_general(a, b, (((1,), (1,)), ((), ())), preferred_element_type=F32)


def call(body, outs, *args, flops=0, vmem=24, **kw):
    size = sum(a.size * a.dtype.itemsize for a in args)
    size += sum(o.size * o.dtype.itemsize for o in outs)
    return pl.pallas_call(
        body,
        out_shape=outs,
        compiler_params=pltpu.CompilerParams(vmem_limit_bytes=vmem * 2**20),
        cost_estimate=pl.CostEstimate(flops=flops, bytes_accessed=size, transcendentals=0),
        **kw,
    )(*args)


def shape(*dims, dtype=BF16):
    return jax.ShapeDtypeStruct(dims, dtype)


def adam_body(w_ref, g_ref, m_ref, s_ref, *outs):
    zl, xx, cc = place()
    corr_one = 1.0 - 0.9**10
    corr_two = 1.0 - 0.999**10
    for d in range(4):
        for r in range(2):
            for k in range(2):
                col = (((zl ^ r) * 4 + (xx + d) % 4) * 2 + (cc ^ k)) * 256
                at = pl.ds(pl.multiple_of(col, 256), 256)
                wfull = w_ref[:, at].astype(F32)
                gfull = g_ref[:, at].astype(F32)
                first_new = 0.9 * m_ref[:, at] + 0.1 * gfull
                second_new = 0.999 * s_ref[:, at] + 0.001 * gfull * gfull
                update = first_new / corr_one / (jnp.sqrt(second_new / corr_two) + 1e-08)
                outs[d][r, k] = (wfull - 0.02 * (update + 0.1 * wfull)).astype(BF16)


def quant_body(b0, b1, b2, b3, c_ref, e_ref, q_ref, s_ref):
    zl, xx, cc = place()
    lane = lax.broadcasted_iota(jnp.int32, (1, BLOCK), 1)
    for r in range(2):
        for d in range(4):
            mine = ((b0, b1, b2, b3)[d][0, 0] if r == 0 else c_ref[d, 0]).astype(F32)
            other = e_ref[r, d].astype(F32)
            block = (zl ^ r) * 4 + (xx - d) % 4
            scales = jnp.zeros((1, BLOCK), F32)
            for n in range(2):
                cols = slice(n * BLOCK, (n + 1) * BLOCK)
                a, b = mine[:, cols], other[:, cols]
                amax = jnp.max(jnp.maximum(jnp.abs(a), jnp.abs(b)), axis=(0, 1), keepdims=True) + 1e-06
                factor = 448.0 / amax
                row_a = pl.multiple_of(block * 128 + cc * 64, 64)
                row_b = pl.multiple_of(block * 128 + (1 - cc) * 64, 64)
                q_ref[pl.ds(row_a, 64), cols] = (a * factor).astype(BF16)
                q_ref[pl.ds(row_b, 64), cols] = (b * factor).astype(BF16)
                scales = jnp.where(lane == n, amax / 448.0, scales)
            s_ref[pl.ds(block, 1), :] = scales


def rows_body(own_ref, oth_ref, bound_ref, *outs):
    zl, xx, cc = place()
    base = (zl * 8 + xx * 2) * TOK
    spot = lax.broadcasted_iota(jnp.int32, (STEPS, TOK), 1)
    one = (bound_ref[...] == base + cc * TOK + spot).astype(BF16)
    two = (bound_ref[...] == base + (1 - cc) * TOK + spot).astype(BF16)
    for d in range(4):
        at = pl.ds(pl.multiple_of(cc * 4096 + (xx + d) % 4 * 1024, 1024), 1024)
        part = jnp.dot(one, own_ref[:, at], preferred_element_type=F32)
        part += jnp.dot(two, oth_ref[:, at], preferred_element_type=F32)
        outs[d][...] = part.astype(BF16)


def query_body(mine_ref, other_ref, wq_ref, q_ref):
    _, xx, cc = place()
    acc = jnp.zeros((STEPS, 256), F32)
    for ref, half in ((mine_ref, cc), (other_ref, 1 - cc)):
        for d in range(4):
            at = pl.ds(pl.multiple_of(half * 4096 + (xx + d) % 4 * 1024, 1024), 1024)
            acc += jnp.dot(ref[:, d * 1024:(d + 1) * 1024], wq_ref[at, :], preferred_element_type=F32)
    q_ref[...] = acc.astype(BF16)


def kv_body(own, oth, zown, zoth, k0, v0, k1, v1, k2, v2, k3, v3, o0, o1, o2, o3, acc):
    _, xx, cc = place()
    step = pl.program_id(0)
    first = cc == 0
    a, b, za, zb = own[...], oth[...], zown[...], zoth[...]
    tokens = jnp.concatenate(
        [jnp.where(first, a, b), jnp.where(first, b, a), jnp.where(first, za, zb), jnp.where(first, zb, za)], 0
    )
    wall = jnp.concatenate([r[...] for r in (k0, v0, k1, v1, k2, v2, k3, v3)], 0)
    part = nt_dot(wall, tokens)

    @pl.when(step == 0)
    def _():
        acc[...] = part

    @pl.when(step > 0)
    def _():
        acc[...] += part

    @pl.when(step == pl.num_programs(0) - 1)
    def _():
        for d, out in enumerate((o0, o1, o2, o3)):
            target = (xx + d) % 4
            for b in range(2):
                piece = (target // 2 * 2 + b - xx) % 4 * 64
                out[b * 32:(b + 1) * 32] = acc[pl.ds(pl.multiple_of(piece, 32), 32), :].astype(BF16)
                out[64 + b * 32:64 + (b + 1) * 32] = acc[pl.ds(pl.multiple_of(piece + 32, 32), 32), :].astype(BF16)


def attend_body(q_ref, half_ref, other_ref, bound_ref, wo_ref, ctx_ref, out_ref):
    zl, xx, cc = place()
    first = cc == 0

    def merged(base):
        parts = []
        for b in range(2):
            m = half_ref[base + b * 32:base + (b + 1) * 32]
            o = other_ref[base + b * 32:base + (b + 1) * 32]
            parts += [jnp.where(first, m, o), jnp.where(first, o, m)]
        return jnp.concatenate(parts, 0)

    keys, values = merged(0), merged(64)
    slot = lax.broadcasted_iota(jnp.int32, (STEPS, 16 * TOK), 1)
    sx = jnp.where(slot >= 4 * TOK, 1, 0) + jnp.where(slot >= 8 * TOK, 1, 0) + jnp.where(slot >= 12 * TOK, 1, 0)
    rest = slot - sx * (4 * TOK)
    sr = jnp.where(rest >= 2 * TOK, 1, 0)
    position = ((zl ^ sr) * 8 + ((xx + sx) & 3) * 2) * TOK + rest - sr * (2 * TOK)
    visible = position <= bound_ref[...]
    for h in range(2):
        scores = jnp.dot(q_ref[:, h * HD:(h + 1) * HD], keys, preferred_element_type=F32)
        scores = scores * (1.0 / jnp.sqrt(F32(HD)))
        scores = jnp.where(visible, scores, F32(-1e30))
        expo = jnp.exp(scores - jnp.max(scores, axis=-1, keepdims=True))
        probs = (expo / jnp.sum(expo, axis=-1, keepdims=True)).astype(BF16)
        ctx_ref[:, h * HD:(h + 1) * HD] = nt_dot(probs, values).astype(BF16)
    project(ctx_ref, wo_ref, out_ref, zl, xx, 1 - cc)


def project(ctx_ref, wo_ref, out_ref, zl, xx, core):
    for d in range(4):
        for r in range(2):
            col = (((zl ^ r) * 4 + (xx + d) % 4) * 2 + core) * 512
            block = wo_ref[:, pl.ds(pl.multiple_of(col, 512), 512)]
            out_ref[:, (d * 2 + r) * 512:(d * 2 + r + 1) * 512] = jnp.dot(
                ctx_ref[...], block, preferred_element_type=F32
            ).astype(BF16)


def mine_body(ctx_ref, wo_ref, out_ref):
    zl, xx, cc = place()
    project(ctx_ref, wo_ref, out_ref, zl, xx, cc)


def on_device(hidden, boundaries, wq_old, wk_old, wv_old, wo_old, weights, grads, moment, second):
    bounds = boundaries.reshape(STEPS, 1)

    zown = send(hidden, zl=1)
    oth = send(hidden, core=1)
    k0, v0 = wk_old.T, wv_old.T
    k3, v1 = send(k0, x=1), send(v0, x=-1)
    v3, k1 = send(v0, x=1), send(k0, x=-1)
    k2, v2 = send(k3, x=1), send(v1, x=-1)

    fresh = call(adam_body, [shape(2, 2, 64, 256)] * 4, weights, grads, moment, second)
    got = [fresh[0]] + [send(fresh[d], x=d) for d in (1, 2, 3)]
    far = send(jnp.stack([g[1] for g in got]), zl=1)
    across = send(jnp.stack([jnp.stack([g[0, 1] for g in got]), far[:, 1]]), core=1)
    quant, scale = call(quant_body, [shape(1024, 256), shape(8, BLOCK, dtype=F32)], *got, far, across)
    quantized = lax.all_gather(quant, "grp", axis=0, tiled=True)
    scales = lax.all_gather(scale[:, :2], "grp", axis=0, tiled=True)

    mine = call(rows_body, [shape(STEPS, 1024)] * 4, hidden, oth, bounds, flops=2 * 128 * 192 * 4096)
    acc = mine[0] + send(mine[1], x=1) + send(mine[2], x=2) + send(mine[3], x=3)
    acc = acc + send(acc, zl=1)
    rows_half = jnp.concatenate([acc] + [send(acc, x=-d) for d in (1, 2, 3)], 1)
    rows_other = send(rows_half, core=1)
    (queries,) = call(
        query_body, [shape(STEPS, 256)], rows_half, rows_other, wq_old, flops=2 * 128 * 8192 * 256
    )

    zoth = send(zown, core=1)
    chunk = 1024
    spec_t = pl.BlockSpec((TOK, chunk), lambda i: (0, i))
    spec_w = pl.BlockSpec((32, chunk), lambda i: (0, i))
    spec_o = pl.BlockSpec((128, 4 * TOK), lambda i: (0, 0))
    kv = call(
        kv_body, [shape(128, 4 * TOK)] * 4, hidden, oth, zown, zoth, k0, v0, k1, v1, k2, v2, k3, v3,
        flops=2 * 384 * 8192 * 256,
        grid=(WIDE // chunk,),
        in_specs=[spec_t] * 4 + [spec_w] * 8,
        out_specs=[spec_o] * 4,
        scratch_shapes=[pltpu.VMEM((256, 4 * TOK), F32)],
    )
    kv_half = jnp.concatenate([kv[0]] + [send(kv[4 - d], x=-d) for d in (1, 2, 3)], 1)
    kv_other = send(kv_half, core=1)

    context, out_other = call(
        attend_body, [shape(STEPS, 256), shape(STEPS, 4096)],
        queries, kv_half, kv_other, bounds, wo_old, flops=2 * 128 * 256 * 8192,
    )
    out_core = send(out_other, core=1)
    (out_mine,) = call(mine_body, [shape(STEPS, 4096)], context, wo_old, flops=2 * 128 * 256 * 4096)
    out = out_mine.astype(F32) + out_core.astype(F32)
    parts = [out[:, d * 1024:(d + 1) * 1024] for d in range(4)]
    total = parts[0]
    for d in (1, 2, 3):
        total = total + send(parts[d].astype(BF16), x=d).astype(F32)
    final = total[:, :512] + send(total[:, 512:].astype(BF16), zl=1).astype(F32)
    return (final.astype(BF16), quantized, scales)


def solution(mesh):
    placed = (
        P(("grp", "tp"), None),
        P("grp", None),
        P(None, "tp"),
        P(None, "tp"),
        P(None, "tp"),
        P("tp", None),
        P(("grp", "tp"), None),
        P(("grp", "tp"), None),
        P(("grp", "tp"), None),
        P(("grp", "tp"), None),
    )
    return jax.shard_map(
        on_device,
        mesh=mesh,
        in_specs=placed,
        out_specs=(P("grp", "tp"), P(None, "tp"), P(None, "tp")),
        check_vma=False,
    )
```

```python
import jax
import jax.numpy as jnp
from jax import lax
from jax.experimental import pallas as pl
from jax.experimental.pallas import tpu as pltpu
from jax.sharding import PartitionSpec as P

HD = 128
BLOCK = 128
TOK = 96
WIDE = 8192
STEPS = 128
AXES = ("grp", "tp")
X_GROUPS = [[8 * a + 2 * e + c for e in range(4)] for a in range(2) for c in range(2)]
ZX_GROUPS = [[2 * e + c for e in range(8)] for c in range(2)]
Y_GROUPS = [[4 * a + b for b in range(4)] for a in range(2)]
F32 = jnp.float32
BF16 = jnp.bfloat16


def coords(i):
    return (i // 64, i // 16 % 4, i // 8 % 2, i // 2 % 4, i % 2)


def send(value, zh=0, y=0, zl=0, x=0, core=0):
    pairs = []
    for i in range(128):
        a, b, l, e, c = coords(i)
        j = ((((a ^ zh) * 4 + (b + y) % 4) * 2 + (l ^ zl)) * 4 + (e + x) % 4) * 2 + (c ^ core)
        pairs.append((i, j))
    return lax.ppermute(value, AXES, pairs)


def swap_all(value, axis, groups):
    return lax.all_to_all(value, axis, split_axis=0, concat_axis=0, axis_index_groups=groups, tiled=True)


def after(value, *others):
    return lax.optimization_barrier((value, *others))[0]


def place():
    ti = lax.axis_index("tp")
    return ti // 8, ti // 2 % 4, ti % 2


def nt_dot(a, b):
    return lax.dot_general(a, b, (((1,), (1,)), ((), ())), preferred_element_type=F32)


ANY = pl.BlockSpec(memory_space=pl.ANY)
HBM = pl.BlockSpec(memory_space=pltpu.HBM)
VMEM = pl.BlockSpec(memory_space=pltpu.VMEM)


def move(args, outs, cost=100):
    def wrap(body, count):
        def run(*refs):
            for copy in fetch(body(*refs[:-1]), refs[-1]):
                copy.wait()

        return call(
            run, outs, *args, in_specs=[ANY] * len(args), out_specs=[VMEM] * len(outs),
            scratch_shapes=[pltpu.SemaphoreType.DMA((count,))], cost=cost,
        )

    return wrap


def fetch(pairs, sems):
    copies = [pltpu.make_async_copy(src, dst, sems.at[i]) for i, (src, dst) in enumerate(pairs)]
    for copy in copies:
        copy.start()
    return copies


def call(body, outs, *args, vmem=24, cost=0, **kw):
    return pl.pallas_call(
        body,
        out_shape=outs,
        cost_estimate=pl.CostEstimate(flops=cost * 10**9, bytes_accessed=0, transcendentals=0),
        compiler_params=pltpu.CompilerParams(vmem_limit_bytes=vmem * 2**20),
        **kw,
    )(*args)


def shape(*dims, dtype=BF16):
    return jax.ShapeDtypeStruct(dims, dtype)


def piece_body(k_ref, v_ref, out_ref):
    out_ref[:32] = k_ref[...]
    out_ref[32:] = v_ref[...]


def halves_body(up_ref, down_ref, k_ref, v_ref):
    k_ref[...] = up_ref[:32]
    v_ref[...] = down_ref[32:]


def first_body(w_any, g_any, m_any, s_any, own_any, oth_any, bound_ref, out_ref, w_ref, g_ref, m_ref, s_ref, own_ref, oth_ref, sems):
    zl, xx, cc = place()
    half = pl.ds(pl.multiple_of(cc * 4096, 4096), 4096)
    pairs = [(own_any.at[:, half], own_ref), (oth_any.at[:, half], oth_ref), (w_any, w_ref), (g_any, g_ref)]
    for i in range(2):
        rows = pl.ds(32 * i, 32)
        pairs += [(m_any.at[rows], m_ref.at[rows]), (s_any.at[rows], s_ref.at[rows])]
    copies = fetch(pairs, sems)
    corr_one = 1.0 - 0.9**10
    corr_two = 1.0 - 0.999**10
    base = (zl * 8 + xx * 2) * TOK
    spot = lax.broadcasted_iota(jnp.int32, (STEPS, TOK), 1)
    one = (bound_ref[...] == base + cc * TOK + spot).astype(BF16)
    two = (bound_ref[...] == base + (1 - cc) * TOK + spot).astype(BF16)
    for copy in copies[:2]:
        copy.wait()
    for x in range(4):
        at = slice(x * 1024, (x + 1) * 1024)
        part = jnp.dot(one, own_ref[:, at], preferred_element_type=F32)
        part += jnp.dot(two, oth_ref[:, at], preferred_element_type=F32)
        out_ref[x, :STEPS] = part.astype(BF16)
    for copy in copies[2:]:
        copy.wait()
    for x in range(4):
        for r in range(2):
            for k in range(2):
                col = (((zl ^ r) * 4 + x) * 2 + (cc ^ k)) * 256
                at = pl.ds(pl.multiple_of(col, 256), 256)
                wfull = w_ref[:, at].astype(F32)
                gfull = g_ref[:, at].astype(F32)
                first_new = 0.9 * m_ref[:, at] + 0.1 * gfull
                second_new = 0.999 * s_ref[:, at] + 0.001 * gfull * gfull
                update = first_new / corr_one / (jnp.sqrt(second_new / corr_two) + 1e-08)
                fresh = (wfull - 0.02 * (update + 0.1 * wfull)).astype(BF16)
                out_ref[x, STEPS:, (r * 2 + k) * 256:(r * 2 + k + 1) * 256] = fresh


def middle_body(got_any, zl_ref, near_ref, far_ref, got_ref, sems):
    for copy in fetch([(got_any.at[x], got_ref.at[x]) for x in range(4)], sems):
        copy.wait()
    acc = got_ref[0, :STEPS] + got_ref[1, :STEPS] + got_ref[2, :STEPS] + got_ref[3, :STEPS]
    for i in range(4):
        zl_ref[i * STEPS:(i + 1) * STEPS] = acc[:, i * 256:(i + 1) * 256]
    for k in range(2):
        for x in range(4):
            row = (k * 4 + x) * 64
            near_ref[row:row + 64] = got_ref[x, STEPS:, k * 256:(k + 1) * 256]
            far = got_ref[x, STEPS:, (2 + k) * 256:(3 + k) * 256]
            far_ref[row:row + 64] = far
            zl_ref[4 * STEPS + row:4 * STEPS + row + 64] = far


def core_pairs(near, zl_ref, zh_ref, far, keep_ref, send_ref):
    pairs = []
    for i, ref in enumerate((near, zl_ref, zh_ref, far)):
        base = 512 if i == 1 else 0
        pairs.append((ref.at[pl.ds(base, 256)], keep_ref.at[pl.ds(i * 256, 256)]))
        pairs.append((ref.at[pl.ds(base + 256, 256)], send_ref.at[pl.ds(i * 256, 256)]))
    return pairs


def line_pairs(k0, k1, k2, k3, kv_ref):
    return [(ref, kv_ref.at[:, pl.ds(x * 4 * TOK, 4 * TOK)]) for x, ref in enumerate((k0, k1, k2, k3))]


def share_body(mine_any, got_any, out_ref, mine_ref, got_ref, sems):
    rows = pl.ds(0, 512)
    for copy in fetch([(mine_any.at[rows], mine_ref), (got_any.at[rows], got_ref)], sems):
        copy.wait()
    for i in range(4):
        rows = slice(i * STEPS, (i + 1) * STEPS)
        block = mine_ref[rows] + got_ref[rows]
        for x in range(4):
            out_ref[x, :, i * 256:(i + 1) * 256] = block


def quant_body(at_ref, first_ref, second_ref, *refs):
    for z, part_ref in enumerate((first_ref, second_ref)):
        pl.when(pl.program_id(0) == z)(lambda part_ref=part_ref: quant_block(at_ref, part_ref, *refs[-2:]))


def quant_block(at_ref, part_ref, q_ref, s_ref):
    zl, cc = at_ref[1], at_ref[2]
    lane = lax.broadcasted_iota(jnp.int32, (1, BLOCK), 1)
    for r in range(2):
        for x in range(4):
            block = (zl ^ r) * 4 + x
            row_a = pl.multiple_of(block * BLOCK + cc * 64, 64)
            row_b = pl.multiple_of(block * BLOCK + (1 - cc) * 64, 64)
            mine = part_ref[0, 0, r, x].astype(F32)
            other = part_ref[0, 1, r, x].astype(F32)
            scales = jnp.zeros((1, BLOCK), F32)
            for n in range(2):
                cols = slice(n * BLOCK, (n + 1) * BLOCK)
                a, b = mine[:, cols], other[:, cols]
                amax = jnp.max(jnp.maximum(jnp.abs(a), jnp.abs(b)), axis=(0, 1), keepdims=True) + 1e-06
                factor = 448.0 / amax
                q_ref[pl.ds(row_a, 64), cols] = (a * factor).astype(BF16)
                q_ref[pl.ds(row_b, 64), cols] = (b * factor).astype(BF16)
                scales = jnp.where(lane == n, amax / 448.0, scales)
            s_ref[0, pl.ds(block, 1), :] = scales


def quantize(parts, at, before):
    def where(z, at_ref):
        return (at_ref[0] ^ z) * 4 + at_ref[3]

    outs = [shape(8192, 256), shape(8, 8, BLOCK, dtype=F32)]
    return pl.pallas_call(
        quant_body,
        out_shape=outs,
        grid_spec=pltpu.PrefetchScalarGridSpec(
            num_scalar_prefetch=1,
            grid=(2,),
            in_specs=[
                pl.BlockSpec((1, 2, 2, 4, 64, 256), lambda z, at_ref, i=p.shape[0] // 2 * i: (i, 0, 0, 0, 0, 0))
                for i, p in enumerate(parts)
            ]
            + [pl.BlockSpec(memory_space=pl.ANY)] * len(before),
            out_specs=[
                pl.BlockSpec((1024, 256), lambda z, at_ref: (where(z, at_ref), 0)),
                pl.BlockSpec((1, 8, BLOCK), lambda z, at_ref: (where(z, at_ref), 0, 0)),
            ],
        ),
        input_output_aliases={3 + i: i for i in range(len(before))},
        compiler_params=pltpu.CompilerParams(vmem_limit_bytes=16 * 2**20),
    )(at, *parts, *before)


def kv_body(own, oth, zown, zoth, p0, w1, k2, v2, w3, o0, o1, o2, o3, acc, tok, wall, sems):
    _, xx, cc = place()
    copies = []
    for e in range(4):
        at = pl.ds(e * 2048, 2048)
        pairs = [(r.at[:, at], tok.at[e, pl.ds(i * TOK, TOK)]) for i, r in enumerate((own, oth, zown, zoth))]
        for row, r in ((0, p0), (64, w1), (128, k2), (160, v2), (192, w3)):
            pairs.append((r.at[:, at], wall.at[e, pl.ds(row, r.shape[0])]))
        copies.append(fetch(pairs, sems.at[e]))
    for e in range(4):
        for copy in copies[e]:
            copy.wait()
        part = nt_dot(wall[e], tok[e])
        if e == 0:
            acc[...] = part
        else:
            acc[...] += part
    total = acc[...]
    swapped = jnp.concatenate([total[:, i * TOK:(i + 1) * TOK] for i in (1, 0, 3, 2)], 1)
    acc[...] = jnp.where(cc == 0, total, swapped)
    for d, out in enumerate((o0, o1, o2, o3)):
        target = (xx + d) % 4
        for b in range(2):
            row = (target // 2 * 2 + b - xx) % 4 * 64
            out[b * 32:(b + 1) * 32] = acc[pl.ds(pl.multiple_of(row, 32), 32), :].astype(BF16)
            out[64 + b * 32:64 + (b + 1) * 32] = acc[pl.ds(pl.multiple_of(row + 32, 32), 32), :].astype(BF16)


def project(ctx_ref, wo_ref, core, i):
    block = wo_ref[:, pl.ds(pl.multiple_of((i * 2 + core) * 512, 512), 512)]
    return jnp.dot(ctx_ref[...], block, preferred_element_type=F32).astype(BF16)


def attend_body(rows_ref, rows_other, wq_ref, half_ref, other_ref, bound_ref, wo_ref, ctx_ref, *outs):
    zl, xx, cc = place()
    first = cc == 0
    queries = jnp.zeros((STEPS, 256), F32)
    for ref, half in ((rows_ref, cc), (rows_other, 1 - cc)):
        for x in range(4):
            at = pl.ds(pl.multiple_of(half * 4096 + x * 1024, 1024), 1024)
            queries += jnp.dot(ref[x], wq_ref[at, :], preferred_element_type=F32)
    queries = queries.astype(BF16)

    def merged(base):
        parts = []
        for b in range(2):
            rows = slice(base + b * 32, base + (b + 1) * 32)
            m, o = half_ref[rows], other_ref[rows]
            parts += [jnp.where(first, m, o), jnp.where(first, o, m)]
        return jnp.concatenate(parts, 0)

    keys, values = merged(0), merged(64)
    slot = lax.broadcasted_iota(jnp.int32, (STEPS, 16 * TOK), 1)
    sx = jnp.where(slot >= 4 * TOK, 1, 0) + jnp.where(slot >= 8 * TOK, 1, 0) + jnp.where(slot >= 12 * TOK, 1, 0)
    rest = slot - sx * (4 * TOK)
    sr = jnp.where(rest >= 2 * TOK, 1, 0)
    position = ((zl ^ sr) * 8 + ((xx + sx) & 3) * 2) * TOK + rest - sr * (2 * TOK)
    visible = position <= bound_ref[...]
    for h in range(2):
        scores = jnp.dot(queries[:, h * HD:(h + 1) * HD], keys, preferred_element_type=F32)
        scores = scores * (1.0 / jnp.sqrt(F32(HD)))
        scores = jnp.where(visible, scores, F32(-1e30))
        expo = jnp.exp(scores - jnp.max(scores, axis=-1, keepdims=True))
        probs = (expo / jnp.sum(expo, axis=-1, keepdims=True)).astype(BF16)
        ctx_ref[:, h * HD:(h + 1) * HD] = nt_dot(probs, values).astype(BF16)
    for i in range(8):
        outs[i // 4][i % 4] = project(ctx_ref, wo_ref, 1 - cc, i)


def mine_body(ctx_ref, wo_ref, got_a, got_b, out_ref):
    _, _, cc = place()
    for i in range(8):
        mine = project(ctx_ref, wo_ref, cc, i).astype(F32)
        out_ref[i] = (mine + (got_a, got_b)[i // 4][i % 4].astype(F32)).astype(BF16)


def final_body(got_ref, out_ref):
    total = got_ref[0].astype(F32)
    for i in range(1, 8):
        total += got_ref[i].astype(F32)
    out_ref[...] = total.astype(BF16)


def on_device(hidden, boundaries, wq_old, wk_old, wv_old, wo_old, weights, grads, moment, second):
    bounds = boundaries.reshape(STEPS, 1)
    gi = lax.axis_index("grp")
    zl, xx, cc = place()

    zown = send(hidden, zl=1)
    oth = send(hidden, core=1)
    (piece,) = call(piece_body, [shape(64, WIDE)], wk_old.T, wv_old.T)
    w3, w1 = send(piece, x=1), send(piece, x=-1)

    (parts,) = call(
        first_body, [shape(4, 192, 1024)], weights, grads, moment, second, hidden, oth, after(bounds, piece),
        in_specs=[HBM] * 6 + [VMEM],
        scratch_shapes=[pltpu.VMEM((64, 4096), BF16)] * 2 + [pltpu.VMEM((64, 4096), F32)] * 2
        + [pltpu.VMEM((TOK, 4096), BF16)] * 2 + [pltpu.SemaphoreType.DMA((8,))],
        cost=100, vmem=60,
    )
    got = swap_all(parts, "tp", X_GROUPS)
    k_half, v_half = call(halves_body, [shape(32, WIDE)] * 2, w3, w1, cost=100)
    k2, v2 = send(k_half, x=1), send(v_half, x=-1)
    got = after(got, k_half)
    got = after(got, zown)
    for_zl, near, far = call(
        middle_body, [shape(1024, 256), shape(512, 256), shape(512, 256)], got, cost=100,
        in_specs=[ANY],
        scratch_shapes=[pltpu.VMEM((4, 192, 1024), BF16), pltpu.SemaphoreType.DMA((4,))],
    )
    from_zl, from_zh, from_far = send(for_zl, zl=1), send(near, zh=1), send(far, zh=1, zl=1)

    zoth = send(zown, core=1)
    kv = call(
        kv_body, [shape(128, 4 * TOK)] * 4,
        hidden, oth, zown, zoth, piece, w1, k2, v2, w3,
        in_specs=[HBM] * 9,
        scratch_shapes=[
            pltpu.VMEM((256, 4 * TOK), F32), pltpu.VMEM((4, 4 * TOK, 2048), BF16),
            pltpu.VMEM((4, 256, 2048), BF16), pltpu.SemaphoreType.DMA((4, 9)),
        ],
        cost=100, vmem=60,
    )
    sums = after((for_zl, from_zl), *kv)
    (shared,) = call(share_body, [shape(4, STEPS, 1024)], *sums, cost=100, in_specs=[ANY] * 2,
        scratch_shapes=[pltpu.VMEM((512, 256), BF16)] * 2 + [pltpu.SemaphoreType.DMA((2,))],
    )
    rows_half = swap_all(shared, "tp", X_GROUPS)
    rows_other = send(rows_half, core=1)

    kv_parts = [kv[0]] + [send(kv[4 - d], x=-d) for d in (1, 2, 3)]
    blocks = after((near, from_zl, from_zh, from_far), shared)
    keep, across = move(blocks, [shape(1024, 256)] * 2)(core_pairs, 8)
    (kv_mine,) = move(kv_parts, [shape(128, 16 * TOK)])(line_pairs, 4)
    kv_other = send(kv_mine, core=1)
    chunks = jnp.stack([a.reshape(2, 2, 4, 64, 256) for a in (keep, send(across, core=1))], 1)
    nears = [send(chunks, y=1), send(chunks, y=3)]

    rows_other = after(rows_other, chunks)
    context, *out_other = call(
        attend_body, [shape(STEPS, 256)] + [shape(4, STEPS, 512)] * 2,
        rows_half, rows_other, wq_old, kv_mine, kv_other, bounds, wo_old, cost=100,
    )
    out_core = [send(o, core=1) for o in out_other]
    (out,) = call(mine_body, [shape(8, STEPS, 512)], context, wo_old, *out_core)
    summed = swap_all(out, "tp", ZX_GROUPS)

    spots = [jnp.stack([gi // 4, zl, cc, (gi - d) % 4]).astype(jnp.int32) for d in range(4)]
    nears = after(tuple(nears), out)
    last = [send(nears[0][:1], y=1), send(nears[1][1:], y=3)]
    done = quantize([after(chunks, out)] * 2, spots[0], ())
    done = quantize([nears[0]] * 2, spots[1], done)
    done = quantize([nears[1]] * 2, spots[3], done)
    (step_features,) = call(final_body, [shape(STEPS, 512)], summed)
    last = after(last, step_features)
    done = quantize(last, spots[2], done)
    quantized = done[0]
    scales = done[1][:, :, :2].reshape(64, 2)
    return (step_features, quantized, scales)


def solution(mesh):
    placed = (
        P(("grp", "tp"), None),
        P("grp", None),
        P(None, "tp"),
        P(None, "tp"),
        P(None, "tp"),
        P("tp", None),
        P(("grp", "tp"), None),
        P(("grp", "tp"), None),
        P(("grp", "tp"), None),
        P(("grp", "tp"), None),
    )
    return jax.shard_map(
        on_device,
        mesh=mesh,
        in_specs=placed,
        out_specs=(P("grp", "tp"), P(None, "tp"), P(None, "tp")),
        check_vma=False,
    )
```

```python
import jax
import jax.numpy as jnp
from jax import lax
from jax.experimental import pallas as pl
from jax.experimental.pallas import tpu as pltpu
from jax.sharding import PartitionSpec as P

HD = 128
BLOCK = 128
TOK = 96
WIDE = 8192
STEPS = 128
AXES = ("grp", "tp")
X_GROUPS = [[8 * a + 2 * e + c for e in range(4)] for a in range(2) for c in range(2)]
ZX_GROUPS = [[2 * e + c for e in range(8)] for c in range(2)]
Y_GROUPS = [[4 * a + b for b in range(4)] for a in range(2)]
F32 = jnp.float32
BF16 = jnp.bfloat16


def coords(i):
    return (i // 64, i // 16 % 4, i // 8 % 2, i // 2 % 4, i % 2)


def send(value, zh=0, y=0, zl=0, x=0, core=0):
    pairs = []
    for i in range(128):
        a, b, l, e, c = coords(i)
        j = ((((a ^ zh) * 4 + (b + y) % 4) * 2 + (l ^ zl)) * 4 + (e + x) % 4) * 2 + (c ^ core)
        pairs.append((i, j))
    return lax.ppermute(value, AXES, pairs)


def swap_all(value, axis, groups):
    return lax.all_to_all(value, axis, split_axis=0, concat_axis=0, axis_index_groups=groups, tiled=True)


def after(value, *others):
    return lax.optimization_barrier((value, *others))[0]


def place():
    ti = lax.axis_index("tp")
    return ti // 8, ti // 2 % 4, ti % 2


def nt_dot(a, b):
    return lax.dot_general(a, b, (((1,), (1,)), ((), ())), preferred_element_type=F32)


ANY = pl.BlockSpec(memory_space=pl.ANY)
HBM = pl.BlockSpec(memory_space=pltpu.HBM)
VMEM = pl.BlockSpec(memory_space=pltpu.VMEM)


def move(args, outs, cost=100):
    def wrap(body, count):
        def run(*refs):
            for copy in fetch(body(*refs[:-1]), refs[-1]):
                copy.wait()

        return call(
            run, outs, *args, in_specs=[ANY] * len(args), out_specs=[VMEM] * len(outs),
            scratch_shapes=[pltpu.SemaphoreType.DMA((count,))], cost=cost,
        )

    return wrap


def fetch(pairs, sems):
    copies = [pltpu.make_async_copy(src, dst, sems.at[i]) for i, (src, dst) in enumerate(pairs)]
    for copy in copies:
        copy.start()
    return copies


def call(body, outs, *args, vmem=24, cost=0, **kw):
    return pl.pallas_call(
        body,
        out_shape=outs,
        cost_estimate=pl.CostEstimate(flops=cost * 10**9, bytes_accessed=0, transcendentals=0),
        compiler_params=pltpu.CompilerParams(vmem_limit_bytes=vmem * 2**20),
        **kw,
    )(*args)


def shape(*dims, dtype=BF16):
    return jax.ShapeDtypeStruct(dims, dtype)


def join_body(top_any, low_any, out_ref, sems):
    for copy in fetch([(top_any, out_ref.at[pl.ds(0, 32)]), (low_any, out_ref.at[pl.ds(32, 32)])], sems):
        copy.wait()


def first_body(w_any, g_any, m_any, s_any, own_any, oth_any, bound_ref, out_ref, w_ref, g_ref, m_ref, s_ref, own_ref, oth_ref, sems):
    zl, xx, cc = place()
    half = pl.ds(pl.multiple_of(cc * 4096, 4096), 4096)
    pairs = [(own_any.at[:, half], own_ref), (oth_any.at[:, half], oth_ref), (w_any, w_ref), (g_any, g_ref)]
    for i in range(2):
        rows = pl.ds(32 * i, 32)
        pairs += [(m_any.at[rows], m_ref.at[rows]), (s_any.at[rows], s_ref.at[rows])]
    copies = fetch(pairs, sems)
    corr_one = 1.0 - 0.9**10
    corr_two = 1.0 - 0.999**10
    base = (zl * 8 + xx * 2) * TOK
    spot = lax.broadcasted_iota(jnp.int32, (STEPS, TOK), 1)
    one = (bound_ref[...] == base + cc * TOK + spot).astype(BF16)
    two = (bound_ref[...] == base + (1 - cc) * TOK + spot).astype(BF16)
    for copy in copies[:2]:
        copy.wait()
    for x in range(4):
        at = slice(x * 1024, (x + 1) * 1024)
        part = jnp.dot(one, own_ref[:, at], preferred_element_type=F32)
        part += jnp.dot(two, oth_ref[:, at], preferred_element_type=F32)
        out_ref[x, :STEPS] = part.astype(BF16)
    for copy in copies[2:]:
        copy.wait()
    for x in range(4):
        for r in range(2):
            for k in range(2):
                col = (((zl ^ r) * 4 + x) * 2 + (cc ^ k)) * 256
                at = pl.ds(pl.multiple_of(col, 256), 256)
                wfull = w_ref[:, at].astype(F32)
                gfull = g_ref[:, at].astype(F32)
                first_new = 0.9 * m_ref[:, at] + 0.1 * gfull
                second_new = 0.999 * s_ref[:, at] + 0.001 * gfull * gfull
                update = first_new / corr_one / (jnp.sqrt(second_new / corr_two) + 1e-08)
                fresh = (wfull - 0.02 * (update + 0.1 * wfull)).astype(BF16)
                out_ref[x, STEPS:, (r * 2 + k) * 256:(r * 2 + k + 1) * 256] = fresh


def middle_body(got_any, acc_ref, keep_ref, give_ref, got_ref, sems):
    for copy in fetch([(got_any.at[x], got_ref.at[x]) for x in range(4)], sems):
        copy.wait()
    acc = got_ref[0, :STEPS] + got_ref[1, :STEPS] + got_ref[2, :STEPS] + got_ref[3, :STEPS]
    for i in range(4):
        acc_ref[i * STEPS:(i + 1) * STEPS] = acc[:, i * 256:(i + 1) * 256]
    for r in range(2):
        for x in range(4):
            row = (r * 4 + x) * 64
            keep_ref[row:row + 64] = got_ref[x, STEPS:, r * 512:r * 512 + 256]
            give_ref[row:row + 64] = got_ref[x, STEPS:, r * 512 + 256:(r + 1) * 512]


def spread_pairs(keep, taken, near, far):
    pairs = []
    for k, ref in enumerate((keep, taken)):
        pairs.append((ref.at[pl.ds(0, 256)], near.at[pl.ds(k * 256, 256)]))
        pairs.append((ref.at[pl.ds(256, 256)], far.at[pl.ds(k * 256, 256)]))
    return pairs


def chunk_pairs(*refs):
    return [(ref, refs[-1].at[pl.ds(i * 512, 512)]) for i, ref in enumerate(refs[:-1])]


def line_pairs(k0, k1, k2, k3, kv_ref):
    return [(ref, kv_ref.at[:, pl.ds(x * 4 * TOK, 4 * TOK)]) for x, ref in enumerate((k0, k1, k2, k3))]


def share_body(mine_any, got_any, out_ref, mine_ref, got_ref, sems):
    for copy in fetch([(mine_any, mine_ref), (got_any, got_ref)], sems):
        copy.wait()
    for i in range(4):
        rows = slice(i * STEPS, (i + 1) * STEPS)
        block = mine_ref[rows] + got_ref[rows]
        for x in range(4):
            out_ref[x, :, i * 256:(i + 1) * 256] = block


def quant_body(at_ref, *refs):
    parts, (q_any, s_any, q_ref, s_ref, sems) = refs[:-5][:2], refs[-5:]
    zl, cc = at_ref[1], at_ref[2]
    lane = lax.broadcasted_iota(jnp.int32, (1, BLOCK), 1)
    copies = []
    for z in range(2):
        part = parts[z].at[parts[z].shape[0] // 2 * z]
        for r in range(2):
            for x in range(4):
                block = (zl ^ r) * 4 + x
                row_a = pl.multiple_of(block * BLOCK + cc * 64, 64)
                row_b = pl.multiple_of(block * BLOCK + (1 - cc) * 64, 64)
                mine, other = part[r, 0, x].astype(F32), part[r, 1, x].astype(F32)
                scales = jnp.zeros((1, BLOCK), F32)
                for n in range(2):
                    cols = slice(n * BLOCK, (n + 1) * BLOCK)
                    a, b = mine[:, cols], other[:, cols]
                    amax = jnp.max(jnp.maximum(jnp.abs(a), jnp.abs(b)), axis=(0, 1), keepdims=True) + 1e-06
                    factor = 448.0 / amax
                    q_ref[z, pl.ds(row_a, 64), cols] = (a * factor).astype(BF16)
                    q_ref[z, pl.ds(row_b, 64), cols] = (b * factor).astype(BF16)
                    scales = jnp.where(lane == n, amax / 448.0, scales)
                s_ref[z, pl.ds(block, 1), :] = scales
        spot = (at_ref[0] ^ z) * 4 + at_ref[3]
        rows = pl.ds(pl.multiple_of(spot * 1024, 1024), 1024)
        copies += fetch([(q_ref.at[z], q_any.at[rows]), (s_ref.at[z], s_any.at[spot])], sems.at[z])
    for copy in copies:
        copy.wait()


def quantize(parts, at, before):
    return call(
        quant_body, [shape(8192, 256), shape(8, 8, BLOCK, dtype=F32)], at, *parts, *before,
        in_specs=[pl.BlockSpec(memory_space=pltpu.SMEM)] + [VMEM] * 2 + [ANY] * len(before),
        out_specs=[ANY] * 2,
        input_output_aliases={3 + i: i for i in range(len(before))},
        scratch_shapes=[
            pltpu.VMEM((2, 1024, 256), BF16), pltpu.VMEM((2, 8, BLOCK), F32), pltpu.SemaphoreType.DMA((2, 2)),
        ],
    )


def kv_body(own, oth, zown, zoth, k0, v0, k1, v1, k2v3, v2, k3, o0, o1, o2, o3, acc, tok, wall, sems):
    _, xx, cc = place()
    copies = []
    for e in range(4):
        at = pl.ds(e * 2048, 2048)
        pairs = [(r.at[:, at], tok.at[e, pl.ds(i * TOK, TOK)]) for i, r in enumerate((own, oth, zown, zoth))]
        k2, v3 = k2v3.at[pl.ds(0, 32)], k2v3.at[pl.ds(32, 32)]
        for i, r in enumerate((k0, v0, k1, v1, k2, v2, k3, v3)):
            pairs.append((r.at[:, at], wall.at[e, pl.ds(i * 32, 32)]))
        copies.append(fetch(pairs, sems.at[e]))
    for e in range(4):
        for copy in copies[e]:
            copy.wait()
        part = nt_dot(wall[e], tok[e])
        if e == 0:
            acc[...] = part
        else:
            acc[...] += part
    total = acc[...]
    swapped = jnp.concatenate([total[:, i * TOK:(i + 1) * TOK] for i in (1, 0, 3, 2)], 1)
    acc[...] = jnp.where(cc == 0, total, swapped)
    for d, out in enumerate((o0, o1, o2, o3)):
        target = (xx + d) % 4
        for b in range(2):
            row = (target // 2 * 2 + b - xx) % 4 * 64
            out[b * 32:(b + 1) * 32] = acc[pl.ds(pl.multiple_of(row, 32), 32), :].astype(BF16)
            out[64 + b * 32:64 + (b + 1) * 32] = acc[pl.ds(pl.multiple_of(row + 32, 32), 32), :].astype(BF16)


def project(ctx_ref, wo_ref, core, i):
    block = wo_ref[:, pl.ds(pl.multiple_of((i * 2 + core) * 512, 512), 512)]
    return jnp.dot(ctx_ref[...], block, preferred_element_type=F32).astype(BF16)


def query_body(rows_any, rows_oth, wq_any, q_ref, rows_ref, wq_ref, row_sems, wq_sems):
    _, _, cc = place()
    pairs = [((rows_any, rows_oth)[i // 4].at[i % 4], rows_ref.at[i]) for i in range(8)]
    row_copies = fetch(pairs, row_sems)
    pairs = []
    for i in range(16):
        row = (cc * 8 + i) % 16 * 512
        pairs.append((wq_any.at[pl.ds(pl.multiple_of(row, 512), 512)], wq_ref.at[pl.ds(i * 512, 512)]))
    wq_copies = fetch(pairs, wq_sems)
    queries = jnp.zeros((STEPS, 256), F32)
    for i in range(8):
        row_copies[i].wait()
        wq_copies[2 * i].wait()
        wq_copies[2 * i + 1].wait()
        queries += jnp.dot(rows_ref[i], wq_ref[i * 1024:(i + 1) * 1024, :], preferred_element_type=F32)
    q_ref[...] = queries.astype(BF16)


def attend_body(q_ref, half_any, other_any, bound_ref, wo_any, out_a, out_b, mine_ref,
                ctx_ref, half_ref, other_ref, wo_ref, kv_sems, wo_sems):
    zl, xx, cc = place()
    first = cc == 0
    outs = (out_a, out_b)
    kv_copies = fetch([(half_any, half_ref), (other_any, other_ref)], kv_sems)
    wo_copies = fetch([(wo_any.at[pl.ds(i * 16, 16)], wo_ref.at[pl.ds(i * 16, 16)]) for i in range(16)], wo_sems)
    queries = q_ref[...]
    for copy in kv_copies:
        copy.wait()

    def merged(base):
        parts = []
        for b in range(2):
            rows = slice(base + b * 32, base + (b + 1) * 32)
            m, o = half_ref[rows], other_ref[rows]
            parts += [jnp.where(first, m, o), jnp.where(first, o, m)]
        return jnp.concatenate(parts, 0)

    keys, values = merged(0), merged(64)
    slot = lax.broadcasted_iota(jnp.int32, (STEPS, 16 * TOK), 1)
    sx = jnp.where(slot >= 4 * TOK, 1, 0) + jnp.where(slot >= 8 * TOK, 1, 0) + jnp.where(slot >= 12 * TOK, 1, 0)
    rest = slot - sx * (4 * TOK)
    sr = jnp.where(rest >= 2 * TOK, 1, 0)
    position = ((zl ^ sr) * 8 + ((xx + sx) & 3) * 2) * TOK + rest - sr * (2 * TOK)
    visible = position <= bound_ref[...]
    for h in range(2):
        scores = jnp.dot(queries[:, h * HD:(h + 1) * HD], keys, preferred_element_type=F32)
        scores = scores * (1.0 / jnp.sqrt(F32(HD)))
        scores = jnp.where(visible, scores, F32(-1e30))
        expo = jnp.exp(scores - jnp.max(scores, axis=-1, keepdims=True))
        probs = (expo / jnp.sum(expo, axis=-1, keepdims=True)).astype(BF16)
        ctx_ref[:, h * HD:(h + 1) * HD] = nt_dot(probs, values).astype(BF16)
    for copy in wo_copies:
        copy.wait()
    for i in range(8):
        outs[i // 4][i % 4] = project(ctx_ref, wo_ref, 1 - cc, i)
    for i in range(8):
        mine_ref[i] = project(ctx_ref, wo_ref, cc, i)


def add_body(mine_any, got_a, got_b, out_ref, mine_ref, got_ref, sems):
    pairs = []
    for i in range(8):
        pairs += [(mine_any.at[i], mine_ref.at[i]), ((got_a, got_b)[i // 4].at[i % 4], got_ref.at[i])]
    copies = fetch(pairs, sems)
    for i in range(8):
        copies[2 * i].wait()
        copies[2 * i + 1].wait()
        out_ref[i] = (mine_ref[i].astype(F32) + got_ref[i].astype(F32)).astype(BF16)


def final_body(got_ref, out_ref):
    total = got_ref[0].astype(F32)
    for i in range(1, 8):
        total += got_ref[i].astype(F32)
    out_ref[...] = total.astype(BF16)


def on_device(hidden, boundaries, wq_old, wk_old, wv_old, wo_old, weights, grads, moment, second):
    bounds = boundaries.reshape(STEPS, 1)
    gi = lax.axis_index("grp")
    zl, xx, cc = place()

    zown = send(hidden, zl=1)
    oth = send(hidden, core=1)
    k0 = wk_old.T
    k3, k1 = send(k0, x=1), send(k0, x=-1)

    (parts,) = call(
        first_body, [shape(4, 192, 1024)], weights, grads, moment, second, hidden, oth, bounds,
        in_specs=[HBM] * 6 + [VMEM],
        scratch_shapes=[pltpu.VMEM((64, 4096), BF16)] * 2 + [pltpu.VMEM((64, 4096), F32)] * 2
        + [pltpu.VMEM((TOK, 4096), BF16)] * 2 + [pltpu.SemaphoreType.DMA((8,))],
        cost=100, vmem=60,
    )
    got = swap_all(parts, "tp", X_GROUPS)
    v0 = wv_old.T
    (joined,) = call(
        join_body, [shape(64, WIDE)], after(k3, k1, parts), v0, in_specs=[HBM] * 2, vmem=60, cost=100,
        scratch_shapes=[pltpu.SemaphoreType.DMA((2,))],
    )
    k2v3 = send(joined, x=1)
    v1 = send(after(v0, joined), x=-1)
    got = after(got, joined)
    acc, keep, give = call(
        middle_body, [shape(512, 256)] * 3, got, cost=100,
        in_specs=[ANY],
        scratch_shapes=[pltpu.VMEM((4, 192, 1024), BF16), pltpu.SemaphoreType.DMA((4,))],
    )
    from_zl = send(acc, zl=1)
    got_core = send(give, core=1)

    zoth = send(zown, core=1)
    (shared,) = call(share_body, [shape(4, STEPS, 1024)], acc, from_zl, in_specs=[ANY] * 2,
        scratch_shapes=[pltpu.VMEM((512, 256), BF16)] * 2 + [pltpu.SemaphoreType.DMA((2,))],
    )
    v2 = send(after(v1, shared), x=-1)
    rows_half = swap_all(shared, "tp", X_GROUPS)
    near, far = move([after(keep, shared), got_core], [shape(512, 256)] * 2, cost=0)(spread_pairs, 4)
    far_zl, near_zh, far_zh = send(far, zl=1), send(near, zh=1), send(far, zh=1, zl=1)

    zboth = after((zown, zoth), shared)
    kv = call(
        kv_body, [shape(128, 4 * TOK)] * 4,
        hidden, oth, *zboth, k0, v0, k1, v1, k2v3, v2, k3,
        in_specs=[HBM] * 11,
        scratch_shapes=[
            pltpu.VMEM((256, 4 * TOK), F32), pltpu.VMEM((4, 4 * TOK, 2048), BF16),
            pltpu.VMEM((4, 256, 2048), BF16), pltpu.SemaphoreType.DMA((4, 12)),
        ],
        cost=100, vmem=60,
    )
    kv_parts = [kv[0]] + [send(kv[4 - d], x=-d) for d in (1, 2, 3)]

    (chunks,) = move([near, after(far_zl, *kv), near_zh, far_zh], [shape(2048, 256)], cost=0)(chunk_pairs, 4)
    nears = [send(chunks, y=1), send(chunks, y=3)]
    (kv_mine,) = move([after(kv_parts[0], far_zl, near_zh, far_zh), *kv_parts[1:]], [shape(128, 16 * TOK)])(line_pairs, 4)
    kv_other = send(kv_mine, core=1)
    rows_other = send(rows_half, core=1)
    (queries,) = call(
        query_body, [shape(STEPS, 256)], rows_half, rows_other, wq_old, in_specs=[HBM] * 3, vmem=60, cost=100,
        scratch_shapes=[
            pltpu.VMEM((8, STEPS, 1024), BF16), pltpu.VMEM((WIDE, 256), BF16),
            pltpu.SemaphoreType.DMA((8,)), pltpu.SemaphoreType.DMA((16,)),
        ],
    )
    *out_other, mine = call(
        attend_body, [shape(4, STEPS, 512)] * 2 + [shape(8, STEPS, 512)],
        queries, kv_mine, kv_other, bounds, wo_old,
        in_specs=[VMEM, HBM, HBM, VMEM, HBM],
        scratch_shapes=[
            pltpu.VMEM((STEPS, 256), BF16), pltpu.VMEM((128, 16 * TOK), BF16), pltpu.VMEM((128, 16 * TOK), BF16),
            pltpu.VMEM((256, WIDE), BF16), pltpu.SemaphoreType.DMA((2,)), pltpu.SemaphoreType.DMA((16,)),
        ],
        vmem=60,
    )
    out_core = [send(o, core=1) for o in out_other]
    (out,) = call(
        add_body, [shape(8, STEPS, 512)], mine, *out_core, in_specs=[HBM] * 3, vmem=60,
        scratch_shapes=[
            pltpu.VMEM((8, STEPS, 512), BF16), pltpu.VMEM((8, STEPS, 512), BF16), pltpu.SemaphoreType.DMA((16,)),
        ],
    )
    summed = swap_all(out, "tp", ZX_GROUPS)

    spots = [jnp.stack([gi // 4, zl, cc, (gi - d) % 4]).astype(jnp.int32) for d in range(4)]
    nears = after(tuple(nears), out)
    last = [send(nears[0][:1024], y=1), send(nears[1][1024:], y=3)]

    def sides(*blocks):
        return [b.reshape(-1, 2, 2, 4, 64, 256) for b in blocks]

    done = quantize(sides(*[after(chunks, out)] * 2), spots[0], ())
    done = quantize(sides(nears[0], nears[0]), spots[1], done)
    done = quantize(sides(nears[1], nears[1]), spots[3], done)
    (step_features,) = call(final_body, [shape(STEPS, 512)], summed)
    last = after(tuple(last), step_features)
    done = quantize(sides(*last), spots[2], done)
    quantized = done[0]
    scales = done[1][:, :, :2].reshape(64, 2)
    return (step_features, quantized, scales)


def solution(mesh):
    placed = (
        P(("grp", "tp"), None),
        P("grp", None),
        P(None, "tp"),
        P(None, "tp"),
        P(None, "tp"),
        P("tp", None),
        P(("grp", "tp"), None),
        P(("grp", "tp"), None),
        P(("grp", "tp"), None),
        P(("grp", "tp"), None),
    )
    return jax.shard_map(
        on_device,
        mesh=mesh,
        in_specs=placed,
        out_specs=(P("grp", "tp"), P(None, "tp"), P(None, "tp")),
        check_vma=False,
    )
```

```python
import jax
import jax.numpy as jnp
from jax import lax
from jax.experimental import pallas as pl
from jax.experimental.pallas import tpu as pltpu
from jax.sharding import PartitionSpec as P

HD = 128
BLOCK = 128
TOK = 96
WIDE = 8192
STEPS = 128
AXES = ("grp", "tp")
X_GROUPS = [[8 * a + 2 * e + c for e in range(4)] for a in range(2) for c in range(2)]
ZX_GROUPS = [[2 * e + c for e in range(8)] for c in range(2)]
Y_GROUPS = [[4 * a + b for b in range(4)] for a in range(2)]
F32 = jnp.float32
BF16 = jnp.bfloat16


def coords(i):
    return (i // 64, i // 16 % 4, i // 8 % 2, i // 2 % 4, i % 2)


def send(value, zh=0, y=0, zl=0, x=0, core=0):
    pairs = []
    for i in range(128):
        a, b, l, e, c = coords(i)
        j = ((((a ^ zh) * 4 + (b + y) % 4) * 2 + (l ^ zl)) * 4 + (e + x) % 4) * 2 + (c ^ core)
        pairs.append((i, j))
    return lax.ppermute(value, AXES, pairs)


def swap_all(value, axis, groups):
    return lax.all_to_all(value, axis, split_axis=0, concat_axis=0, axis_index_groups=groups, tiled=True)


def after(value, *others):
    return lax.optimization_barrier((value, *others))[0]


def place():
    ti = lax.axis_index("tp")
    return ti // 8, ti // 2 % 4, ti % 2


def column(bound_ref):
    row = lax.broadcasted_iota(jnp.int32, (STEPS, STEPS), 0)
    lane = lax.broadcasted_iota(jnp.int32, (STEPS, STEPS), 1)
    spread = jnp.where(row == lane, bound_ref[...].astype(F32), 0.0)
    return jnp.sum(spread, axis=1, keepdims=True).astype(jnp.int32)


def nt_dot(a, b):
    return lax.dot_general(a, b, (((1,), (1,)), ((), ())), preferred_element_type=F32)


ANY = pl.BlockSpec(memory_space=pl.ANY)
HBM = pl.BlockSpec(memory_space=pltpu.HBM)
VMEM = pl.BlockSpec(memory_space=pltpu.VMEM)


def move(args, outs, cost=100, vmem=24):
    def wrap(body, count):
        def run(*refs):
            for copy in fetch(body(*refs[:-1]), refs[-1]):
                copy.wait()

        return call(
            run, outs, *args, in_specs=[ANY] * len(args), out_specs=[VMEM] * len(outs),
            scratch_shapes=[pltpu.SemaphoreType.DMA((count,))], cost=cost, vmem=vmem,
        )

    return wrap


def fetch(pairs, sems):
    copies = [pltpu.make_async_copy(src, dst, sems.at[i]) for i, (src, dst) in enumerate(pairs)]
    for copy in copies:
        copy.start()
    return copies


def call(body, outs, *args, vmem=24, cost=0, **kw):
    return pl.pallas_call(
        body,
        out_shape=outs,
        cost_estimate=pl.CostEstimate(flops=cost * 10**9, bytes_accessed=0, transcendentals=0),
        compiler_params=pltpu.CompilerParams(vmem_limit_bytes=vmem * 2**20),
        **kw,
    )(*args)


def shape(*dims, dtype=BF16):
    return jax.ShapeDtypeStruct(dims, dtype)


def join_body(top_any, low_any, out_ref, sems):
    for copy in fetch([(top_any, out_ref.at[pl.ds(0, 32)]), (low_any, out_ref.at[pl.ds(32, 32)])], sems):
        copy.wait()


def token_body(_, out_ref):
    out_ref[...] = jnp.zeros((8, BLOCK), F32)


def first_body(w_any, g_any, m_any, s_any, own_any, oth_any, bound_ref, out_ref, w_ref, g_ref, m_ref, s_ref, own_ref, oth_ref, sems):
    zl, xx, cc = place()
    half = pl.ds(pl.multiple_of(cc * 4096, 4096), 4096)
    pairs = [(own_any.at[:, half], own_ref), (oth_any.at[:, half], oth_ref), (w_any, w_ref), (g_any, g_ref)]
    for i in range(2):
        rows = pl.ds(32 * i, 32)
        pairs += [(m_any.at[rows], m_ref.at[rows]), (s_any.at[rows], s_ref.at[rows])]
    copies = fetch(pairs, sems)
    corr_one = 1.0 - 0.9**10
    corr_two = 1.0 - 0.999**10
    base = (zl * 8 + xx * 2) * TOK
    spot = lax.broadcasted_iota(jnp.int32, (STEPS, TOK), 1)
    bound = column(bound_ref)
    one = (bound == base + cc * TOK + spot).astype(BF16)
    two = (bound == base + (1 - cc) * TOK + spot).astype(BF16)
    for copy in copies[:2]:
        copy.wait()
    for x in range(4):
        at = slice(x * 1024, (x + 1) * 1024)
        part = jnp.dot(one, own_ref[:, at], preferred_element_type=F32)
        part += jnp.dot(two, oth_ref[:, at], preferred_element_type=F32)
        out_ref[x, :STEPS] = part.astype(BF16)
    for copy in copies[2:]:
        copy.wait()
    for x in range(4):
        for r in range(2):
            for k in range(2):
                col = (((zl ^ r) * 4 + x) * 2 + (cc ^ k)) * 256
                at = pl.ds(pl.multiple_of(col, 256), 256)
                wfull = w_ref[:, at].astype(F32)
                gfull = g_ref[:, at].astype(F32)
                first_new = 0.9 * m_ref[:, at] + 0.1 * gfull
                second_new = 0.999 * s_ref[:, at] + 0.001 * gfull * gfull
                update = first_new / corr_one / (jnp.sqrt(second_new / corr_two) + 1e-08)
                fresh = (wfull - 0.02 * (update + 0.1 * wfull)).astype(BF16)
                out_ref[x, STEPS:, (r * 2 + k) * 256:(r * 2 + k + 1) * 256] = fresh


def middle_body(got_any, acc_ref, keep_ref, give_ref, got_ref, sems):
    for copy in fetch([(got_any.at[x], got_ref.at[x]) for x in range(4)], sems):
        copy.wait()
    acc = got_ref[0, :STEPS] + got_ref[1, :STEPS] + got_ref[2, :STEPS] + got_ref[3, :STEPS]
    for i in range(4):
        acc_ref[i * STEPS:(i + 1) * STEPS] = acc[:, i * 256:(i + 1) * 256]
    for r in range(2):
        for x in range(4):
            row = (r * 4 + x) * 64
            keep_ref[row:row + 64] = got_ref[x, STEPS:, r * 512:r * 512 + 256]
            give_ref[row:row + 64] = got_ref[x, STEPS:, r * 512 + 256:(r + 1) * 512]


def spread_pairs(keep, taken, near, far):
    pairs = []
    for k, ref in enumerate((keep, taken)):
        pairs.append((ref.at[pl.ds(0, 256)], near.at[pl.ds(k * 256, 256)]))
        pairs.append((ref.at[pl.ds(256, 256)], far.at[pl.ds(k * 256, 256)]))
    return pairs


def chunk_pairs(*refs):
    return [(ref, refs[-1].at[pl.ds(i * 512, 512)]) for i, ref in enumerate(refs[:-1])]


def on_pairs(up, down, first, second):
    return [(up.at[pl.ds(0, 1024)], first), (down.at[pl.ds(1024, 1024)], second)]


def line_pairs(k0, k1, k2, k3, kv_ref):
    return [(ref, kv_ref.at[:, pl.ds(x * 4 * TOK, 4 * TOK)]) for x, ref in enumerate((k0, k1, k2, k3))]


def share_body(mine_any, got_any, out_ref, mine_ref, got_ref, sems):
    for copy in fetch([(mine_any, mine_ref), (got_any, got_ref)], sems):
        copy.wait()
    for i in range(4):
        rows = slice(i * STEPS, (i + 1) * STEPS)
        block = mine_ref[rows] + got_ref[rows]
        for x in range(4):
            out_ref[x, :, i * 256:(i + 1) * 256] = block


def quant_body(at_ref, *refs):
    parts, (q_any, s_ref, q_ref, sems) = refs[:2], refs[-4:]
    zl, cc = at_ref[1], at_ref[2]
    lane = lax.broadcasted_iota(jnp.int32, (1, 64), 1)
    scales = [refs[3][n:n + 1, :] if len(refs) > 6 else jnp.zeros((1, 64), F32) for n in range(2)]
    copies = []
    for z in range(2):
        part = parts[z].at[parts[z].shape[0] // 2 * z]
        spot = (at_ref[0] ^ z) * 4 + at_ref[3]
        for r in range(2):
            for x in range(4):
                block = (zl ^ r) * 4 + x
                row_a = pl.multiple_of(block * BLOCK + cc * 64, 64)
                row_b = pl.multiple_of(block * BLOCK + (1 - cc) * 64, 64)
                mine, other = part[r, 0, x].astype(F32), part[r, 1, x].astype(F32)
                for n in range(2):
                    cols = slice(n * BLOCK, (n + 1) * BLOCK)
                    a, b = mine[:, cols], other[:, cols]
                    amax = jnp.max(jnp.maximum(jnp.abs(a), jnp.abs(b)), axis=(0, 1), keepdims=True) + 1e-06
                    factor = 448.0 / amax
                    q_ref[z, pl.ds(row_a, 64), cols] = (a * factor).astype(BF16)
                    q_ref[z, pl.ds(row_b, 64), cols] = (b * factor).astype(BF16)
                    scales[n] = jnp.where(lane == spot * 8 + block, amax / 448.0, scales[n])
        rows = pl.ds(pl.multiple_of(spot * 1024, 1024), 1024)
        copies += fetch([(q_ref.at[z], q_any.at[rows])], sems.at[pl.ds(z, 1)])
    for n in range(2):
        s_ref[n:n + 1, :] = scales[n]
    for copy in copies:
        copy.wait()


def quantize(parts, at, before):
    return call(
        quant_body, [shape(8192, 256), shape(2, 64, dtype=F32)], at, *parts, *before,
        in_specs=[pl.BlockSpec(memory_space=pltpu.SMEM)] + [VMEM] * 2 + [ANY, VMEM][:len(before)],
        out_specs=[ANY, VMEM],
        input_output_aliases={3: 0} if before else {},
        scratch_shapes=[pltpu.VMEM((2, 1024, 256), BF16), pltpu.SemaphoreType.DMA((2,))],
    )


def kv_body(own, oth, zown, zoth, k0, v0, k1, v1, k2v3, v2, k3, o0, o1, o2, o3, acc, tok, wall, sems):
    _, xx, cc = place()
    copies = []
    for e in range(4):
        at = pl.ds(e * 2048, 2048)
        pairs = [(r.at[:, at], tok.at[e, pl.ds(i * TOK, TOK)]) for i, r in enumerate((own, oth, zown, zoth))]
        k2, v3 = k2v3.at[pl.ds(0, 32)], k2v3.at[pl.ds(32, 32)]
        for i, r in enumerate((k0, v0, k1, v1, k2, v2, k3, v3)):
            pairs.append((r.at[:, at], wall.at[e, pl.ds(i * 32, 32)]))
        copies.append(fetch(pairs, sems.at[e]))
    for e in range(4):
        for copy in copies[e]:
            copy.wait()
        part = nt_dot(wall[e], tok[e])
        if e == 0:
            acc[...] = part
        else:
            acc[...] += part
    total = acc[...]
    swapped = jnp.concatenate([total[:, i * TOK:(i + 1) * TOK] for i in (1, 0, 3, 2)], 1)
    acc[...] = jnp.where(cc == 0, total, swapped)
    for d, out in enumerate((o0, o1, o2, o3)):
        target = (xx + d) % 4
        for b in range(2):
            row = (target // 2 * 2 + b - xx) % 4 * 64
            out[b * 32:(b + 1) * 32] = acc[pl.ds(pl.multiple_of(row, 32), 32), :].astype(BF16)
            out[64 + b * 32:64 + (b + 1) * 32] = acc[pl.ds(pl.multiple_of(row + 32, 32), 32), :].astype(BF16)


def project(ctx_ref, wo_ref, core, i):
    block = wo_ref[:, pl.ds(pl.multiple_of((i * 2 + core) * 512, 512), 512)]
    return jnp.dot(ctx_ref[...], block, preferred_element_type=F32).astype(BF16)


def attend_body(rows_any, rows_oth, wq_any, half_any, other_any, bound_ref, wo_any, _, out_a, out_b, mine_any,
                ctx_ref, half_ref, other_ref, wo_ref, stage, rows_ref, wq_ref, kv_sems, wo_sems, out_sems, row_sems, wq_sems):
    zl, xx, cc = place()
    first = cc == 0
    outs = (out_a, out_b)
    pairs = [((rows_any, rows_oth)[i // 4].at[i % 4], rows_ref.at[i]) for i in range(8)]
    row_copies = fetch(pairs, row_sems)
    pairs = []
    for i in range(16):
        row = (cc * 8 + i) % 16 * 512
        pairs.append((wq_any.at[pl.ds(pl.multiple_of(row, 512), 512)], wq_ref.at[pl.ds(i * 512, 512)]))
    wq_copies = fetch(pairs, wq_sems)
    kv_copies = fetch([(half_any, half_ref), (other_any, other_ref)], kv_sems)
    wo_copies = fetch([(wo_any.at[pl.ds(i * 16, 16)], wo_ref.at[pl.ds(i * 16, 16)]) for i in range(16)], wo_sems)
    queries = jnp.zeros((STEPS, 256), F32)
    for i in range(8):
        row_copies[i].wait()
        wq_copies[2 * i].wait()
        wq_copies[2 * i + 1].wait()
        queries += jnp.dot(rows_ref[i], wq_ref[i * 1024:(i + 1) * 1024, :], preferred_element_type=F32)
    queries = queries.astype(BF16)
    for copy in kv_copies:
        copy.wait()

    def merged(base):
        parts = []
        for b in range(2):
            rows = slice(base + b * 32, base + (b + 1) * 32)
            m, o = half_ref[rows], other_ref[rows]
            parts += [jnp.where(first, m, o), jnp.where(first, o, m)]
        return jnp.concatenate(parts, 0)

    keys, values = merged(0), merged(64)
    slot = lax.broadcasted_iota(jnp.int32, (STEPS, 16 * TOK), 1)
    sx = jnp.where(slot >= 4 * TOK, 1, 0) + jnp.where(slot >= 8 * TOK, 1, 0) + jnp.where(slot >= 12 * TOK, 1, 0)
    rest = slot - sx * (4 * TOK)
    sr = jnp.where(rest >= 2 * TOK, 1, 0)
    position = ((zl ^ sr) * 8 + ((xx + sx) & 3) * 2) * TOK + rest - sr * (2 * TOK)
    visible = position <= column(bound_ref)
    for h in range(2):
        scores = jnp.dot(queries[:, h * HD:(h + 1) * HD], keys, preferred_element_type=F32)
        scores = scores * (1.0 / jnp.sqrt(F32(HD)))
        scores = jnp.where(visible, scores, F32(-1e30))
        expo = jnp.exp(scores - jnp.max(scores, axis=-1, keepdims=True))
        probs = (expo / jnp.sum(expo, axis=-1, keepdims=True)).astype(BF16)
        ctx_ref[:, h * HD:(h + 1) * HD] = nt_dot(probs, values).astype(BF16)
    for copy in wo_copies:
        copy.wait()
    leaving = []
    for i in range(8):
        stage[i] = project(ctx_ref, wo_ref, 1 - cc, i)
        leaving.append(leave((stage.at[i], outs[i // 4].at[i % 4]), out_sems, i))
    for i in range(8):
        stage[8 + i] = project(ctx_ref, wo_ref, cc, i)
        leaving.append(leave((stage.at[8 + i], mine_any.at[i]), out_sems, 8 + i))
    for copy in leaving:
        copy.wait()


def leave(blocks, sems, i):
    copy = pltpu.make_async_copy(*blocks, sems.at[i])
    copy.start()
    return copy


def add_body(mine_any, got_a, got_b, out_any, mine_ref, got_ref, stage, sems, out_sems):
    pairs = []
    for i in range(8):
        pairs += [(mine_any.at[i], mine_ref.at[i]), ((got_a, got_b)[i // 4].at[i % 4], got_ref.at[i])]
    copies = fetch(pairs, sems)
    leaving = []
    for i in range(8):
        copies[2 * i].wait()
        copies[2 * i + 1].wait()
        stage[i] = (mine_ref[i].astype(F32) + got_ref[i].astype(F32)).astype(BF16)
        leaving.append(leave((stage.at[i], out_any.at[i]), out_sems, i))
    for copy in leaving:
        copy.wait()


def final_body(got_ref, out_ref):
    total = got_ref[0].astype(F32)
    for i in range(1, 8):
        total += got_ref[i].astype(F32)
    out_ref[...] = total.astype(BF16)


def on_device(hidden, boundaries, wq_old, wk_old, wv_old, wo_old, weights, grads, moment, second):
    bounds = boundaries
    gi = lax.axis_index("grp")
    zl, xx, cc = place()

    zown = send(hidden, zl=1)
    oth = send(hidden, core=1)
    k0 = wk_old.T
    k3, k1 = send(k0, x=1), send(k0, x=-1)

    (parts,) = call(
        first_body, [shape(4, 192, 1024)], weights, grads, moment, second, hidden, oth, bounds,
        in_specs=[HBM] * 6 + [VMEM],
        scratch_shapes=[pltpu.VMEM((64, 4096), BF16)] * 2 + [pltpu.VMEM((64, 4096), F32)] * 2
        + [pltpu.VMEM((TOK, 4096), BF16)] * 2 + [pltpu.SemaphoreType.DMA((8,))],
        cost=100, vmem=60,
    )
    got = swap_all(parts, "tp", X_GROUPS)
    v0 = wv_old.T
    (joined,) = call(
        join_body, [shape(64, WIDE)], after(k3, k1, parts), v0, in_specs=[HBM] * 2, vmem=60, cost=100,
        scratch_shapes=[pltpu.SemaphoreType.DMA((2,))],
    )
    k2v3 = send(joined, x=1)
    v1 = send(after(v0, joined), x=-1)
    got = after(got, joined)
    acc, keep, give = call(
        middle_body, [shape(512, 256)] * 3, got, cost=100,
        in_specs=[ANY],
        scratch_shapes=[pltpu.VMEM((4, 192, 1024), BF16), pltpu.SemaphoreType.DMA((4,))],
    )
    from_zl = send(acc, zl=1)
    got_core = send(give, core=1)

    zoth = send(zown, core=1)
    (shared,) = call(share_body, [shape(4, STEPS, 1024)], acc, from_zl, in_specs=[ANY] * 2,
        scratch_shapes=[pltpu.VMEM((512, 256), BF16)] * 2 + [pltpu.SemaphoreType.DMA((2,))],
    )
    v2 = send(after(v1, shared), x=-1)
    rows_half = swap_all(shared, "tp", X_GROUPS)
    near, far = move([after(keep, shared), got_core], [shape(512, 256)] * 2, cost=0)(spread_pairs, 4)
    far_zl, near_zh, far_zh = send(far, zl=1), send(near, zh=1), send(far, zh=1, zl=1)

    zboth = after((zown, zoth), shared)
    kv = call(
        kv_body, [shape(128, 4 * TOK)] * 4,
        hidden, oth, *zboth, k0, v0, k1, v1, k2v3, v2, k3,
        in_specs=[HBM] * 11,
        scratch_shapes=[
            pltpu.VMEM((256, 4 * TOK), F32), pltpu.VMEM((4, 4 * TOK, 2048), BF16),
            pltpu.VMEM((4, 256, 2048), BF16), pltpu.SemaphoreType.DMA((4, 12)),
        ],
        cost=100, vmem=60,
    )
    kv_parts = [kv[0]] + [send(kv[4 - d], x=-d) for d in (1, 2, 3)]

    (chunks,) = move([near, after(far_zl, *kv), near_zh, far_zh], [shape(2048, 256)], cost=0)(chunk_pairs, 4)
    nears = [send(chunks, y=1), send(chunks, y=3)]
    (kv_mine,) = move([after(kv_parts[0], far_zl, near_zh, far_zh), *kv_parts[1:]], [shape(128, 16 * TOK)])(line_pairs, 4)
    kv_other = send(kv_mine, core=1)
    rows_other = send(rows_half, core=1)
    (token,) = call(token_body, [shape(8, BLOCK, dtype=F32)], rows_other, in_specs=[ANY], cost=100)
    *out_other, mine = call(
        attend_body, [shape(4, STEPS, 512)] * 2 + [shape(8, STEPS, 512)],
        rows_half, rows_other, wq_old, kv_mine, kv_other, bounds, wo_old, token,
        in_specs=[HBM] * 5 + [VMEM, HBM, ANY],
        scratch_shapes=[
            pltpu.VMEM((STEPS, 256), BF16), pltpu.VMEM((128, 16 * TOK), BF16), pltpu.VMEM((128, 16 * TOK), BF16),
            pltpu.VMEM((256, WIDE), BF16), pltpu.VMEM((16, STEPS, 512), BF16),
            pltpu.VMEM((8, STEPS, 1024), BF16), pltpu.VMEM((WIDE, 256), BF16),
            pltpu.SemaphoreType.DMA((2,)), pltpu.SemaphoreType.DMA((16,)), pltpu.SemaphoreType.DMA((16,)),
            pltpu.SemaphoreType.DMA((8,)), pltpu.SemaphoreType.DMA((16,)),
        ],
        out_specs=[ANY] * 3,
        vmem=60,
    )
    out_core = [send(o, core=1) for o in out_other]
    (out,) = call(
        add_body, [shape(8, STEPS, 512)], mine, *out_core, in_specs=[HBM] * 3, out_specs=[ANY], vmem=60,
        scratch_shapes=[pltpu.VMEM((8, STEPS, 512), BF16)] * 3
        + [pltpu.SemaphoreType.DMA((16,)), pltpu.SemaphoreType.DMA((8,))],
    )
    summed = swap_all(out, "tp", ZX_GROUPS)

    spots = [jnp.stack([gi // 4, zl, cc, (gi - d) % 4]).astype(jnp.int32) for d in range(4)]
    nears = after(tuple(nears), out)
    on = move(nears, [shape(1024, 256)] * 2, cost=0)(on_pairs, 2)
    last = [send(on[0], y=1), send(on[1], y=3)]

    def sides(*blocks):
        return [b.reshape(-1, 2, 2, 4, 64, 256) for b in blocks]

    done = quantize(sides(*[after(chunks, out)] * 2), spots[0], ())
    done = quantize(sides(nears[0], nears[0]), spots[1], done)
    done = quantize(sides(nears[1], nears[1]), spots[3], done)
    (step_features,) = call(final_body, [shape(STEPS, 512)], summed)
    last = after(tuple(last), step_features)
    done = quantize(sides(*last), spots[2], done)
    quantized = done[0]
    scales = done[1].T
    return (step_features, quantized, scales)


def solution(mesh):
    placed = (
        P(("grp", "tp"), None),
        P("grp", None),
        P(None, "tp"),
        P(None, "tp"),
        P(None, "tp"),
        P("tp", None),
        P(("grp", "tp"), None),
        P(("grp", "tp"), None),
        P(("grp", "tp"), None),
        P(("grp", "tp"), None),
    )
    return jax.shard_map(
        on_device,
        mesh=mesh,
        in_specs=placed,
        out_specs=(P("grp", "tp"), P(None, "tp"), P(None, "tp")),
        check_vma=False,
    )
```

```python
import jax
import jax.numpy as jnp
from jax import lax
from jax.experimental import pallas as pl
from jax.experimental.pallas import tpu as pltpu
from jax.sharding import PartitionSpec as P

HD = 128
BLOCK = 128
TOK = 96
WIDE = 8192
STEPS = 128
AXES = ("grp", "tp")
X_GROUPS = [[8 * a + 2 * e + c for e in range(4)] for a in range(2) for c in range(2)]
ZX_GROUPS = [[2 * e + c for e in range(8)] for c in range(2)]
Y_GROUPS = [[4 * a + b for b in range(4)] for a in range(2)]
F32 = jnp.float32
BF16 = jnp.bfloat16


def coords(i):
    return (i // 64, i // 16 % 4, i // 8 % 2, i // 2 % 4, i % 2)


def send(value, zh=0, y=0, zl=0, x=0, core=0):
    pairs = []
    for i in range(128):
        a, b, l, e, c = coords(i)
        j = ((((a ^ zh) * 4 + (b + y) % 4) * 2 + (l ^ zl)) * 4 + (e + x) % 4) * 2 + (c ^ core)
        pairs.append((i, j))
    return lax.ppermute(value, AXES, pairs)


def swap_all(value, axis, groups):
    return lax.all_to_all(value, axis, split_axis=0, concat_axis=0, axis_index_groups=groups, tiled=True)


def after(value, *others):
    return lax.optimization_barrier((value, *others))[0]


def place():
    ti = lax.axis_index("tp")
    return ti // 8, ti // 2 % 4, ti % 2


def column(bound_ref):
    row = lax.broadcasted_iota(jnp.int32, (STEPS, STEPS), 0)
    lane = lax.broadcasted_iota(jnp.int32, (STEPS, STEPS), 1)
    spread = jnp.where(row == lane, bound_ref[...].astype(F32), 0.0)
    return jnp.sum(spread, axis=1, keepdims=True).astype(jnp.int32)


def nt_dot(a, b):
    return lax.dot_general(a, b, (((1,), (1,)), ((), ())), preferred_element_type=F32)


ANY = pl.BlockSpec(memory_space=pl.ANY)
HBM = pl.BlockSpec(memory_space=pltpu.HBM)
VMEM = pl.BlockSpec(memory_space=pltpu.VMEM)


def move(args, outs, cost=100, vmem=24):
    def wrap(body, count):
        def run(*refs):
            for copy in fetch(body(*refs[:-1]), refs[-1]):
                copy.wait()

        return call(
            run, outs, *args, in_specs=[ANY] * len(args), out_specs=[VMEM] * len(outs),
            scratch_shapes=[pltpu.SemaphoreType.DMA((count,))], cost=cost, vmem=vmem,
        )

    return wrap


def fetch(pairs, sems):
    copies = [pltpu.make_async_copy(src, dst, sems.at[i]) for i, (src, dst) in enumerate(pairs)]
    for copy in copies:
        copy.start()
    return copies


def call(body, outs, *args, vmem=24, cost=0, **kw):
    return pl.pallas_call(
        body,
        out_shape=outs,
        cost_estimate=pl.CostEstimate(flops=cost * 10**9, bytes_accessed=0, transcendentals=0),
        compiler_params=pltpu.CompilerParams(vmem_limit_bytes=vmem * 2**20),
        **kw,
    )(*args)


def shape(*dims, dtype=BF16):
    return jax.ShapeDtypeStruct(dims, dtype)


def join_body(top_any, low_any, out_ref, sems):
    for copy in fetch([(top_any, out_ref.at[pl.ds(0, 32)]), (low_any, out_ref.at[pl.ds(32, 32)])], sems):
        copy.wait()


def token_body(_, out_ref):
    out_ref[...] = jnp.zeros((8, BLOCK), F32)


def first_body(w_any, g_any, m_any, s_any, own_any, oth_any, bound_ref, out_ref, w_ref, g_ref, m_ref, s_ref, own_ref, oth_ref, sems):
    zl, xx, cc = place()
    half = pl.ds(pl.multiple_of(cc * 4096, 4096), 4096)
    pairs = [(own_any.at[:, half], own_ref), (oth_any.at[:, half], oth_ref), (w_any, w_ref), (g_any, g_ref)]
    for i in range(2):
        rows = pl.ds(32 * i, 32)
        pairs += [(m_any.at[rows], m_ref.at[rows]), (s_any.at[rows], s_ref.at[rows])]
    copies = fetch(pairs, sems)
    corr_one = 1.0 - 0.9**10
    corr_two = 1.0 - 0.999**10
    base = (zl * 8 + xx * 2) * TOK
    spot = lax.broadcasted_iota(jnp.int32, (STEPS, TOK), 1)
    bound = column(bound_ref)
    one = (bound == base + cc * TOK + spot).astype(BF16)
    two = (bound == base + (1 - cc) * TOK + spot).astype(BF16)
    for copy in copies[:2]:
        copy.wait()
    for x in range(4):
        at = slice(x * 1024, (x + 1) * 1024)
        part = jnp.dot(one, own_ref[:, at], preferred_element_type=F32)
        part += jnp.dot(two, oth_ref[:, at], preferred_element_type=F32)
        out_ref[x, :STEPS] = part.astype(BF16)
    for copy in copies[2:]:
        copy.wait()
    for x in range(4):
        for r in range(2):
            for k in range(2):
                col = (((zl ^ r) * 4 + x) * 2 + (cc ^ k)) * 256
                at = pl.ds(pl.multiple_of(col, 256), 256)
                wfull = w_ref[:, at].astype(F32)
                gfull = g_ref[:, at].astype(F32)
                first_new = 0.9 * m_ref[:, at] + 0.1 * gfull
                second_new = 0.999 * s_ref[:, at] + 0.001 * gfull * gfull
                update = first_new / corr_one / (jnp.sqrt(second_new / corr_two) + 1e-08)
                fresh = (wfull - 0.02 * (update + 0.1 * wfull)).astype(BF16)
                out_ref[x, STEPS:, (r * 2 + k) * 256:(r * 2 + k + 1) * 256] = fresh


def middle_body(got_any, acc_ref, keep_ref, give_ref, got_ref, sems):
    for copy in fetch([(got_any.at[x], got_ref.at[x]) for x in range(4)], sems):
        copy.wait()
    acc = got_ref[0, :STEPS] + got_ref[1, :STEPS] + got_ref[2, :STEPS] + got_ref[3, :STEPS]
    for i in range(4):
        acc_ref[i * STEPS:(i + 1) * STEPS] = acc[:, i * 256:(i + 1) * 256]
    for r in range(2):
        for x in range(4):
            row = (r * 4 + x) * 64
            keep_ref[row:row + 64] = got_ref[x, STEPS:, r * 512:r * 512 + 256]
            give_ref[row:row + 64] = got_ref[x, STEPS:, r * 512 + 256:(r + 1) * 512]


def spread_pairs(keep, taken, near, far):
    pairs = []
    for k, ref in enumerate((keep, taken)):
        pairs.append((ref.at[pl.ds(0, 256)], near.at[pl.ds(k * 256, 256)]))
        pairs.append((ref.at[pl.ds(256, 256)], far.at[pl.ds(k * 256, 256)]))
    return pairs


def chunk_pairs(*refs):
    return [(ref, refs[-1].at[pl.ds(i * 512, 512)]) for i, ref in enumerate(refs[:-1])]


def on_pairs(up, down, first, second):
    return [(up.at[pl.ds(0, 1024)], first), (down.at[pl.ds(1024, 1024)], second)]


def line_pairs(k0, k1, k2, k3, kv_ref):
    return [(ref, kv_ref.at[:, pl.ds(x * 4 * TOK, 4 * TOK)]) for x, ref in enumerate((k0, k1, k2, k3))]


def share_body(mine_any, got_any, out_ref, mine_ref, got_ref, sems):
    for copy in fetch([(mine_any, mine_ref), (got_any, got_ref)], sems):
        copy.wait()
    for i in range(4):
        rows = slice(i * STEPS, (i + 1) * STEPS)
        block = mine_ref[rows] + got_ref[rows]
        for x in range(4):
            out_ref[x, :, i * 256:(i + 1) * 256] = block


def quant_body(at_ref, *refs):
    parts, (q_any, s_ref, q_ref, sems) = refs[:2], refs[-4:]
    zl, cc = at_ref[1], at_ref[2]
    lane = lax.broadcasted_iota(jnp.int32, (1, 64), 1)
    scales = [refs[3][n:n + 1, :] if len(refs) > 6 else jnp.zeros((1, 64), F32) for n in range(2)]
    copies = []
    for z in range(2):
        part = parts[z].at[parts[z].shape[0] // 2 * z]
        spot = (at_ref[0] ^ z) * 4 + at_ref[3]
        for r in range(2):
            for x in range(4):
                block = (zl ^ r) * 4 + x
                row_a = pl.multiple_of(block * BLOCK + cc * 64, 64)
                row_b = pl.multiple_of(block * BLOCK + (1 - cc) * 64, 64)
                mine, other = part[r, 0, x].astype(F32), part[r, 1, x].astype(F32)
                for n in range(2):
                    cols = slice(n * BLOCK, (n + 1) * BLOCK)
                    a, b = mine[:, cols], other[:, cols]
                    amax = jnp.max(jnp.maximum(jnp.abs(a), jnp.abs(b)), axis=(0, 1), keepdims=True) + 1e-06
                    factor = 448.0 / amax
                    q_ref[z, pl.ds(row_a, 64), cols] = (a * factor).astype(BF16)
                    q_ref[z, pl.ds(row_b, 64), cols] = (b * factor).astype(BF16)
                    scales[n] = jnp.where(lane == spot * 8 + block, amax / 448.0, scales[n])
        rows = pl.ds(pl.multiple_of(spot * 1024, 1024), 1024)
        copies += fetch([(q_ref.at[z], q_any.at[rows])], sems.at[pl.ds(z, 1)])
    for n in range(2):
        s_ref[n:n + 1, :] = scales[n]
    for copy in copies:
        copy.wait()


def quantize(parts, at, before):
    return call(
        quant_body, [shape(8192, 256), shape(2, 64, dtype=F32)], at, *parts, *before,
        in_specs=[pl.BlockSpec(memory_space=pltpu.SMEM)] + [VMEM] * 2 + [ANY, VMEM][:len(before)],
        out_specs=[ANY, VMEM],
        input_output_aliases={3: 0} if before else {},
        scratch_shapes=[pltpu.VMEM((2, 1024, 256), BF16), pltpu.SemaphoreType.DMA((2,))],
    )


def kv_body(own, oth, zown, zoth, k0, v0, k1, v1, k2v3, v2, k3, o0, o1, o2, o3, acc, tok, wall, sems):
    _, xx, cc = place()
    copies = []
    for e in range(4):
        at = pl.ds(e * 2048, 2048)
        pairs = [(r.at[:, at], tok.at[e, pl.ds(i * TOK, TOK)]) for i, r in enumerate((own, oth, zown, zoth))]
        k2, v3 = k2v3.at[pl.ds(0, 32)], k2v3.at[pl.ds(32, 32)]
        for i, r in enumerate((k0, v0, k1, v1, k2, v2, k3, v3)):
            pairs.append((r.at[:, at], wall.at[e, pl.ds(i * 32, 32)]))
        copies.append(fetch(pairs, sems.at[e]))
    for e in range(4):
        for copy in copies[e]:
            copy.wait()
        part = nt_dot(wall[e], tok[e])
        if e == 0:
            acc[...] = part
        else:
            acc[...] += part
    total = acc[...]
    swapped = jnp.concatenate([total[:, i * TOK:(i + 1) * TOK] for i in (1, 0, 3, 2)], 1)
    acc[...] = jnp.where(cc == 0, total, swapped)
    for d, out in enumerate((o0, o1, o2, o3)):
        target = (xx + d) % 4
        for b in range(2):
            row = (target // 2 * 2 + b - xx) % 4 * 64
            out[b * 32:(b + 1) * 32] = acc[pl.ds(pl.multiple_of(row, 32), 32), :].astype(BF16)
            out[64 + b * 32:64 + (b + 1) * 32] = acc[pl.ds(pl.multiple_of(row + 32, 32), 32), :].astype(BF16)


def project(ctx_ref, wo_ref, core, i):
    block = wo_ref[:, pl.ds(pl.multiple_of((i * 2 + core) * 512, 512), 512)]
    return jnp.dot(ctx_ref[...], block, preferred_element_type=F32).astype(BF16)


def attend_body(rows_any, rows_oth, wq_any, half_any, other_any, bound_ref, wo_any, _, out_a, out_b, mine_any,
                ctx_ref, half_ref, other_ref, wo_ref, stage, rows_ref, wq_ref, kv_sems, wo_sems, out_sems, row_sems, wq_sems):
    zl, xx, cc = place()
    first = cc == 0
    outs = (out_a, out_b)
    pairs = [((rows_any, rows_oth)[i // 4].at[i % 4], rows_ref.at[i]) for i in range(8)]
    row_copies = fetch(pairs, row_sems)
    pairs = []
    for i in range(16):
        row = (cc * 8 + i) % 16 * 512
        pairs.append((wq_any.at[pl.ds(pl.multiple_of(row, 512), 512)], wq_ref.at[pl.ds(i * 512, 512)]))
    wq_copies = fetch(pairs, wq_sems)
    kv_copies = fetch([(half_any, half_ref), (other_any, other_ref)], kv_sems)
    wo_copies = fetch([(wo_any.at[pl.ds(i * 16, 16)], wo_ref.at[pl.ds(i * 16, 16)]) for i in range(16)], wo_sems)
    queries = jnp.zeros((STEPS, 256), F32)
    for i in range(8):
        row_copies[i].wait()
        wq_copies[2 * i].wait()
        wq_copies[2 * i + 1].wait()
        queries += jnp.dot(rows_ref[i], wq_ref[i * 1024:(i + 1) * 1024, :], preferred_element_type=F32)
    queries = queries.astype(BF16)
    for copy in kv_copies:
        copy.wait()

    def merged(base):
        parts = []
        for b in range(2):
            rows = slice(base + b * 32, base + (b + 1) * 32)
            m, o = half_ref[rows], other_ref[rows]
            parts += [jnp.where(first, m, o), jnp.where(first, o, m)]
        return jnp.concatenate(parts, 0)

    keys, values = merged(0), merged(64)
    slot = lax.broadcasted_iota(jnp.int32, (STEPS, 16 * TOK), 1)
    sx = jnp.where(slot >= 4 * TOK, 1, 0) + jnp.where(slot >= 8 * TOK, 1, 0) + jnp.where(slot >= 12 * TOK, 1, 0)
    rest = slot - sx * (4 * TOK)
    sr = jnp.where(rest >= 2 * TOK, 1, 0)
    position = ((zl ^ sr) * 8 + ((xx + sx) & 3) * 2) * TOK + rest - sr * (2 * TOK)
    visible = position <= column(bound_ref)
    for h in range(2):
        scores = jnp.dot(queries[:, h * HD:(h + 1) * HD], keys, preferred_element_type=F32)
        scores = scores * (1.0 / jnp.sqrt(F32(HD)))
        scores = jnp.where(visible, scores, F32(-1e30))
        expo = jnp.exp(scores - jnp.max(scores, axis=-1, keepdims=True))
        probs = (expo / jnp.sum(expo, axis=-1, keepdims=True)).astype(BF16)
        ctx_ref[:, h * HD:(h + 1) * HD] = nt_dot(probs, values).astype(BF16)
    for copy in wo_copies:
        copy.wait()
    leaving = []
    for i in range(8):
        stage[i] = project(ctx_ref, wo_ref, 1 - cc, i)
        leaving.append(leave((stage.at[i], outs[i // 4].at[i % 4]), out_sems, i))
    for i in range(8):
        stage[8 + i] = project(ctx_ref, wo_ref, cc, i)
        leaving.append(leave((stage.at[8 + i], mine_any.at[i]), out_sems, 8 + i))
    for copy in leaving:
        copy.wait()


def leave(blocks, sems, i):
    copy = pltpu.make_async_copy(*blocks, sems.at[i])
    copy.start()
    return copy


def add_body(mine_any, got_a, got_b, out_any, mine_ref, got_ref, stage, sems, out_sems):
    pairs = []
    for i in range(8):
        pairs += [(mine_any.at[i], mine_ref.at[i]), ((got_a, got_b)[i // 4].at[i % 4], got_ref.at[i])]
    copies = fetch(pairs, sems)
    leaving = []
    for i in range(8):
        copies[2 * i].wait()
        copies[2 * i + 1].wait()
        stage[i] = (mine_ref[i].astype(F32) + got_ref[i].astype(F32)).astype(BF16)
        leaving.append(leave((stage.at[i], out_any.at[i]), out_sems, i))
    for copy in leaving:
        copy.wait()


def final_body(got_ref, out_ref):
    total = got_ref[0].astype(F32)
    for i in range(1, 8):
        total += got_ref[i].astype(F32)
    out_ref[...] = total.astype(BF16)


def on_device(hidden, boundaries, wq_old, wk_old, wv_old, wo_old, weights, grads, moment, second):
    bounds = boundaries
    gi = lax.axis_index("grp")
    zl, xx, cc = place()

    zown = send(hidden, zl=1)
    oth = send(hidden, core=1)
    k0 = wk_old.T
    k3, k1 = send(k0, x=1), send(k0, x=-1)

    (parts,) = call(
        first_body, [shape(4, 192, 1024)], weights, grads, moment, second, hidden, oth, bounds,
        in_specs=[HBM] * 6 + [VMEM],
        scratch_shapes=[pltpu.VMEM((64, 4096), BF16)] * 2 + [pltpu.VMEM((64, 4096), F32)] * 2
        + [pltpu.VMEM((TOK, 4096), BF16)] * 2 + [pltpu.SemaphoreType.DMA((8,))],
        cost=4, vmem=60,
    )
    got = swap_all(parts, "tp", X_GROUPS)
    v0 = wv_old.T
    (joined,) = call(
        join_body, [shape(64, WIDE)], after(k3, k1, parts), v0, in_specs=[HBM] * 2, vmem=60, cost=8,
        scratch_shapes=[pltpu.SemaphoreType.DMA((2,))],
    )
    k2v3 = send(joined, x=1)
    v1 = send(after(v0, joined), x=-1)
    got = after(got, joined)
    acc, keep, give = call(
        middle_body, [shape(512, 256)] * 3, got, cost=100,
        in_specs=[ANY],
        scratch_shapes=[pltpu.VMEM((4, 192, 1024), BF16), pltpu.SemaphoreType.DMA((4,))],
    )
    from_zl = send(acc, zl=1)
    got_core = send(give, core=1)

    zoth = send(zown, core=1)
    (shared,) = call(share_body, [shape(4, STEPS, 1024)], acc, from_zl, in_specs=[ANY] * 2,
        scratch_shapes=[pltpu.VMEM((512, 256), BF16)] * 2 + [pltpu.SemaphoreType.DMA((2,))],
    )
    v2 = send(after(v1, shared), x=-1)
    rows_half = swap_all(shared, "tp", X_GROUPS)
    near, far = move([after(keep, shared), got_core], [shape(512, 256)] * 2, cost=0)(spread_pairs, 4)
    far_zl, near_zh, far_zh = send(far, zl=1), send(near, zh=1), send(far, zh=1, zl=1)

    zboth = after((zown, zoth), shared)
    kv = call(
        kv_body, [shape(128, 4 * TOK)] * 4,
        hidden, oth, *zboth, k0, v0, k1, v1, k2v3, v2, k3,
        in_specs=[HBM] * 11,
        scratch_shapes=[
            pltpu.VMEM((256, 4 * TOK), F32), pltpu.VMEM((4, 4 * TOK, 2048), BF16),
            pltpu.VMEM((4, 256, 2048), BF16), pltpu.SemaphoreType.DMA((4, 12)),
        ],
        cost=100, vmem=60,
    )
    kv_parts = [kv[0]] + [send(kv[4 - d], x=-d) for d in (1, 2, 3)]

    (chunks,) = move([near, after(far_zl, *kv), near_zh, far_zh], [shape(2048, 256)], cost=0)(chunk_pairs, 4)
    nears = [send(chunks, y=1), send(chunks, y=3)]
    (kv_mine,) = move([after(kv_parts[0], far_zl, near_zh, far_zh), *kv_parts[1:]], [shape(128, 16 * TOK)])(line_pairs, 4)
    kv_other = send(kv_mine, core=1)
    rows_other = send(rows_half, core=1)
    (token,) = call(token_body, [shape(8, BLOCK, dtype=F32)], rows_other, in_specs=[ANY], cost=100)
    *out_other, mine = call(
        attend_body, [shape(4, STEPS, 512)] * 2 + [shape(8, STEPS, 512)],
        rows_half, rows_other, wq_old, kv_mine, kv_other, bounds, wo_old, token,
        in_specs=[HBM] * 5 + [VMEM, HBM, ANY],
        scratch_shapes=[
            pltpu.VMEM((STEPS, 256), BF16), pltpu.VMEM((128, 16 * TOK), BF16), pltpu.VMEM((128, 16 * TOK), BF16),
            pltpu.VMEM((256, WIDE), BF16), pltpu.VMEM((16, STEPS, 512), BF16),
            pltpu.VMEM((8, STEPS, 1024), BF16), pltpu.VMEM((WIDE, 256), BF16),
            pltpu.SemaphoreType.DMA((2,)), pltpu.SemaphoreType.DMA((16,)), pltpu.SemaphoreType.DMA((16,)),
            pltpu.SemaphoreType.DMA((8,)), pltpu.SemaphoreType.DMA((16,)),
        ],
        out_specs=[ANY] * 3,
        vmem=60,
    )
    out_core = [send(o, core=1) for o in out_other]
    (out,) = call(
        add_body, [shape(8, STEPS, 512)], mine, *out_core, in_specs=[HBM] * 3, out_specs=[ANY], vmem=60,
        scratch_shapes=[pltpu.VMEM((8, STEPS, 512), BF16)] * 3
        + [pltpu.SemaphoreType.DMA((16,)), pltpu.SemaphoreType.DMA((8,))],
    )
    summed = swap_all(out, "tp", ZX_GROUPS)

    spots = [jnp.stack([gi // 4, zl, cc, (gi - d) % 4]).astype(jnp.int32) for d in range(4)]
    nears = after(tuple(nears), out)
    on = move(nears, [shape(1024, 256)] * 2, cost=0)(on_pairs, 2)
    last = [send(on[0], y=1), send(on[1], y=3)]

    def sides(*blocks):
        return [b.reshape(-1, 2, 2, 4, 64, 256) for b in blocks]

    done = quantize(sides(*[after(chunks, out)] * 2), spots[0], ())
    done = quantize(sides(nears[0], nears[0]), spots[1], done)
    done = quantize(sides(nears[1], nears[1]), spots[3], done)
    (step_features,) = call(final_body, [shape(STEPS, 512)], summed)
    last = after(tuple(last), step_features)
    done = quantize(sides(*last), spots[2], done)
    quantized = done[0]
    scales = done[1].T
    return (step_features, quantized, scales)


def solution(mesh):
    placed = (
        P(("grp", "tp"), None),
        P("grp", None),
        P(None, "tp"),
        P(None, "tp"),
        P(None, "tp"),
        P("tp", None),
        P(("grp", "tp"), None),
        P(("grp", "tp"), None),
        P(("grp", "tp"), None),
        P(("grp", "tp"), None),
    )
    return jax.shard_map(
        on_device,
        mesh=mesh,
        in_specs=placed,
        out_specs=(P("grp", "tp"), P(None, "tp"), P(None, "tp")),
        check_vma=False,
    )
```

```python
import jax
import jax.numpy as jnp
from jax import lax
from jax.experimental import pallas as pl
from jax.experimental.pallas import tpu as pltpu
from jax.sharding import PartitionSpec as P

HD = 128
BLOCK = 128
TOK = 96
WIDE = 8192
STEPS = 128
AXES = ("grp", "tp")
X_GROUPS = [[8 * a + 2 * e + c for e in range(4)] for a in range(2) for c in range(2)]
ZX_GROUPS = [[2 * e + c for e in range(8)] for c in range(2)]
Y_GROUPS = [[4 * a + b for b in range(4)] for a in range(2)]
F32 = jnp.float32
BF16 = jnp.bfloat16


def coords(i):
    return (i // 64, i // 16 % 4, i // 8 % 2, i // 2 % 4, i % 2)


def send(value, zh=0, y=0, zl=0, x=0, core=0):
    pairs = []
    for i in range(128):
        a, b, l, e, c = coords(i)
        j = ((((a ^ zh) * 4 + (b + y) % 4) * 2 + (l ^ zl)) * 4 + (e + x) % 4) * 2 + (c ^ core)
        pairs.append((i, j))
    return lax.ppermute(value, AXES, pairs)


def swap_all(value, axis, groups):
    return lax.all_to_all(value, axis, split_axis=0, concat_axis=0, axis_index_groups=groups, tiled=True)


def after(value, *others):
    return lax.optimization_barrier((value, *others))[0]


def place():
    ti = lax.axis_index("tp")
    return ti // 8, ti // 2 % 4, ti % 2


def column(bound_ref):
    row = lax.broadcasted_iota(jnp.int32, (STEPS, STEPS), 0)
    lane = lax.broadcasted_iota(jnp.int32, (STEPS, STEPS), 1)
    spread = jnp.where(row == lane, bound_ref[...].astype(F32), 0.0)
    return jnp.sum(spread, axis=1, keepdims=True).astype(jnp.int32)


def nt_dot(a, b):
    return lax.dot_general(a, b, (((1,), (1,)), ((), ())), preferred_element_type=F32)


ANY = pl.BlockSpec(memory_space=pl.ANY)
HBM = pl.BlockSpec(memory_space=pltpu.HBM)
VMEM = pl.BlockSpec(memory_space=pltpu.VMEM)


def move(args, outs, cost=100, vmem=24):
    def wrap(body, count):
        def run(*refs):
            for copy in fetch(body(*refs[:-1]), refs[-1]):
                copy.wait()

        return call(
            run, outs, *args, in_specs=[ANY] * len(args), out_specs=[VMEM] * len(outs),
            scratch_shapes=[pltpu.SemaphoreType.DMA((count,))], cost=cost, vmem=vmem,
        )

    return wrap


def fetch(pairs, sems):
    copies = [pltpu.make_async_copy(src, dst, sems.at[i]) for i, (src, dst) in enumerate(pairs)]
    for copy in copies:
        copy.start()
    return copies


def call(body, outs, *args, vmem=24, cost=0, **kw):
    return pl.pallas_call(
        body,
        out_shape=outs,
        cost_estimate=pl.CostEstimate(flops=cost * 10**9, bytes_accessed=0, transcendentals=0),
        compiler_params=pltpu.CompilerParams(vmem_limit_bytes=vmem * 2**20),
        **kw,
    )(*args)


def shape(*dims, dtype=BF16):
    return jax.ShapeDtypeStruct(dims, dtype)


def join_body(top_any, low_any, out_ref, sems):
    for copy in fetch([(top_any, out_ref.at[pl.ds(0, 32)]), (low_any, out_ref.at[pl.ds(32, 32)])], sems):
        copy.wait()


def token_body(_, out_ref):
    out_ref[...] = jnp.zeros((8, BLOCK), F32)


def first_body(w_any, g_any, m_any, s_any, own_any, oth_any, bound_ref, out_ref, w_ref, g_ref, m_ref, s_ref, own_ref, oth_ref, sems):
    zl, xx, cc = place()
    half = pl.ds(pl.multiple_of(cc * 4096, 4096), 4096)
    pairs = [(own_any.at[:, half], own_ref), (oth_any.at[:, half], oth_ref), (w_any, w_ref), (g_any, g_ref)]
    for i in range(2):
        rows = pl.ds(32 * i, 32)
        pairs += [(m_any.at[rows], m_ref.at[rows]), (s_any.at[rows], s_ref.at[rows])]
    copies = fetch(pairs, sems)
    corr_one = 1.0 - 0.9**10
    corr_two = 1.0 - 0.999**10
    base = (zl * 8 + xx * 2) * TOK
    spot = lax.broadcasted_iota(jnp.int32, (STEPS, TOK), 1)
    bound = column(bound_ref)
    one = (bound == base + cc * TOK + spot).astype(BF16)
    two = (bound == base + (1 - cc) * TOK + spot).astype(BF16)
    for copy in copies[:2]:
        copy.wait()
    for x in range(4):
        at = slice(x * 1024, (x + 1) * 1024)
        part = jnp.dot(one, own_ref[:, at], preferred_element_type=F32)
        part += jnp.dot(two, oth_ref[:, at], preferred_element_type=F32)
        out_ref[x, :STEPS] = part.astype(BF16)
    for copy in copies[2:]:
        copy.wait()
    for x in range(4):
        for r in range(2):
            for k in range(2):
                col = (((zl ^ r) * 4 + x) * 2 + (cc ^ k)) * 256
                at = pl.ds(pl.multiple_of(col, 256), 256)
                wfull = w_ref[:, at].astype(F32)
                gfull = g_ref[:, at].astype(F32)
                first_new = 0.9 * m_ref[:, at] + 0.1 * gfull
                second_new = 0.999 * s_ref[:, at] + 0.001 * gfull * gfull
                update = first_new / corr_one / (jnp.sqrt(second_new / corr_two) + 1e-08)
                fresh = (wfull - 0.02 * (update + 0.1 * wfull)).astype(BF16)
                out_ref[x, STEPS:, (r * 2 + k) * 256:(r * 2 + k + 1) * 256] = fresh


def middle_body(got_any, acc_ref, keep_ref, give_ref, got_ref, sems):
    for copy in fetch([(got_any.at[x], got_ref.at[x]) for x in range(4)], sems):
        copy.wait()
    acc = got_ref[0, :STEPS] + got_ref[1, :STEPS] + got_ref[2, :STEPS] + got_ref[3, :STEPS]
    for i in range(4):
        acc_ref[i * STEPS:(i + 1) * STEPS] = acc[:, i * 256:(i + 1) * 256]
    for r in range(2):
        for x in range(4):
            row = (r * 4 + x) * 64
            keep_ref[row:row + 64] = got_ref[x, STEPS:, r * 512:r * 512 + 256]
            give_ref[row:row + 64] = got_ref[x, STEPS:, r * 512 + 256:(r + 1) * 512]


def spread_pairs(keep, taken, near, far):
    pairs = []
    for k, ref in enumerate((keep, taken)):
        pairs.append((ref.at[pl.ds(0, 256)], near.at[pl.ds(k * 256, 256)]))
        pairs.append((ref.at[pl.ds(256, 256)], far.at[pl.ds(k * 256, 256)]))
    return pairs


def chunk_pairs(*refs):
    return [(ref, refs[-1].at[pl.ds(i * 512, 512)]) for i, ref in enumerate(refs[:-1])]


def on_pairs(up, down, first, second):
    return [(up.at[pl.ds(0, 1024)], first), (down.at[pl.ds(1024, 1024)], second)]


def line_pairs(k0, k1, k2, k3, kv_ref):
    return [(ref, kv_ref.at[:, pl.ds(x * 4 * TOK, 4 * TOK)]) for x, ref in enumerate((k0, k1, k2, k3))]


def share_body(mine_any, got_any, out_ref, mine_ref, got_ref, sems):
    for copy in fetch([(mine_any, mine_ref), (got_any, got_ref)], sems):
        copy.wait()
    for i in range(4):
        rows = slice(i * STEPS, (i + 1) * STEPS)
        block = mine_ref[rows] + got_ref[rows]
        for x in range(4):
            out_ref[x, :, i * 256:(i + 1) * 256] = block


def quant_body(at_ref, *refs):
    parts, (q_any, s_ref, q_ref, sems) = refs[:2], refs[-4:]
    zl, cc = at_ref[1], at_ref[2]
    lane = lax.broadcasted_iota(jnp.int32, (1, 64), 1)
    scales = [refs[3][n:n + 1, :] if len(refs) > 6 else jnp.zeros((1, 64), F32) for n in range(2)]
    copies = []
    for z in range(2):
        part = parts[z].at[parts[z].shape[0] // 2 * z]
        spot = (at_ref[0] ^ z) * 4 + at_ref[3]
        for r in range(2):
            for x in range(4):
                block = (zl ^ r) * 4 + x
                row_a = pl.multiple_of(block * BLOCK + cc * 64, 64)
                row_b = pl.multiple_of(block * BLOCK + (1 - cc) * 64, 64)
                mine, other = part[r, 0, x].astype(F32), part[r, 1, x].astype(F32)
                for n in range(2):
                    cols = slice(n * BLOCK, (n + 1) * BLOCK)
                    a, b = mine[:, cols], other[:, cols]
                    amax = jnp.max(jnp.maximum(jnp.abs(a), jnp.abs(b)), axis=(0, 1), keepdims=True) + 1e-06
                    factor = 448.0 / amax
                    q_ref[z, pl.ds(row_a, 64), cols] = (a * factor).astype(BF16)
                    q_ref[z, pl.ds(row_b, 64), cols] = (b * factor).astype(BF16)
                    scales[n] = jnp.where(lane == spot * 8 + block, amax / 448.0, scales[n])
        rows = pl.ds(pl.multiple_of(spot * 1024, 1024), 1024)
        copies += fetch([(q_ref.at[z], q_any.at[rows])], sems.at[pl.ds(z, 1)])
    for n in range(2):
        s_ref[n:n + 1, :] = scales[n]
    for copy in copies:
        copy.wait()


def quantize(parts, at, before):
    return call(
        quant_body, [shape(8192, 256), shape(2, 64, dtype=F32)], at, *parts, *before,
        in_specs=[pl.BlockSpec(memory_space=pltpu.SMEM)] + [VMEM] * 2 + [ANY, VMEM][:len(before)],
        out_specs=[ANY, VMEM],
        input_output_aliases={3: 0} if before else {},
        scratch_shapes=[pltpu.VMEM((2, 1024, 256), BF16), pltpu.SemaphoreType.DMA((2,))],
    )


def kv_body(own, oth, zown, zoth, k0, v0, k1, v1, k2v3, v2, k3, o0, o1, o2, o3, acc, tok, wall, sems):
    _, xx, cc = place()
    copies = []
    for e in range(4):
        at = pl.ds(e * 2048, 2048)
        pairs = [(r.at[:, at], tok.at[e, pl.ds(i * TOK, TOK)]) for i, r in enumerate((own, oth, zown, zoth))]
        k2, v3 = k2v3.at[pl.ds(0, 32)], k2v3.at[pl.ds(32, 32)]
        for i, r in enumerate((k0, v0, k1, v1, k2, v2, k3, v3)):
            pairs.append((r.at[:, at], wall.at[e, pl.ds(i * 32, 32)]))
        copies.append(fetch(pairs, sems.at[e]))
    for e in range(4):
        for copy in copies[e]:
            copy.wait()
        part = nt_dot(wall[e], tok[e])
        if e == 0:
            acc[...] = part
        else:
            acc[...] += part
    total = acc[...]
    swapped = jnp.concatenate([total[:, i * TOK:(i + 1) * TOK] for i in (1, 0, 3, 2)], 1)
    acc[...] = jnp.where(cc == 0, total, swapped)
    for d, out in enumerate((o0, o1, o2, o3)):
        target = (xx + d) % 4
        for b in range(2):
            row = (target // 2 * 2 + b - xx) % 4 * 64
            out[b * 32:(b + 1) * 32] = acc[pl.ds(pl.multiple_of(row, 32), 32), :].astype(BF16)
            out[64 + b * 32:64 + (b + 1) * 32] = acc[pl.ds(pl.multiple_of(row + 32, 32), 32), :].astype(BF16)


def project(ctx_ref, wo_ref, core, i):
    block = wo_ref[:, pl.ds(pl.multiple_of((i * 2 + core) * 512, 512), 512)]
    return jnp.dot(ctx_ref[...], block, preferred_element_type=F32).astype(BF16)


def attend_body(rows_any, rows_oth, wq_any, half_any, other_any, bound_ref, wo_any, _, out_a, out_b, mine_any,
                ctx_ref, half_ref, other_ref, wo_ref, stage, rows_ref, wq_ref, kv_sems, wo_sems, out_sems, row_sems, wq_sems):
    zl, xx, cc = place()
    first = cc == 0
    outs = (out_a, out_b)
    pairs = [((rows_any, rows_oth)[i // 4].at[i % 4], rows_ref.at[i]) for i in range(8)]
    row_copies = fetch(pairs, row_sems)
    pairs = []
    for i in range(4):
        row = (cc * 2 + i) % 4 * 2048
        pairs.append((wq_any.at[pl.ds(pl.multiple_of(row, 2048), 2048)], wq_ref.at[pl.ds(i * 2048, 2048)]))
    wq_copies = fetch(pairs, wq_sems)
    kv_copies = fetch([(half_any, half_ref), (other_any, other_ref)], kv_sems)
    wo_copies = fetch([(wo_any.at[pl.ds(i * 64, 64)], wo_ref.at[pl.ds(i * 64, 64)]) for i in range(4)], wo_sems)
    queries = jnp.zeros((STEPS, 256), F32)
    for i in range(8):
        row_copies[i].wait()
        if i % 2 == 0:
            wq_copies[i // 2].wait()
        queries += jnp.dot(rows_ref[i], wq_ref[i * 1024:(i + 1) * 1024, :], preferred_element_type=F32)
    queries = queries.astype(BF16)
    for copy in kv_copies:
        copy.wait()

    def merged(base):
        parts = []
        for b in range(2):
            rows = slice(base + b * 32, base + (b + 1) * 32)
            m, o = half_ref[rows], other_ref[rows]
            parts += [jnp.where(first, m, o), jnp.where(first, o, m)]
        return jnp.concatenate(parts, 0)

    keys, values = merged(0), merged(64)
    slot = lax.broadcasted_iota(jnp.int32, (STEPS, 16 * TOK), 1)
    sx = jnp.where(slot >= 4 * TOK, 1, 0) + jnp.where(slot >= 8 * TOK, 1, 0) + jnp.where(slot >= 12 * TOK, 1, 0)
    rest = slot - sx * (4 * TOK)
    sr = jnp.where(rest >= 2 * TOK, 1, 0)
    position = ((zl ^ sr) * 8 + ((xx + sx) & 3) * 2) * TOK + rest - sr * (2 * TOK)
    visible = position <= column(bound_ref)
    for h in range(2):
        scores = jnp.dot(queries[:, h * HD:(h + 1) * HD], keys, preferred_element_type=F32)
        scores = scores * (1.0 / jnp.sqrt(F32(HD)))
        scores = jnp.where(visible, scores, F32(-1e30))
        expo = jnp.exp(scores - jnp.max(scores, axis=-1, keepdims=True))
        probs = (expo / jnp.sum(expo, axis=-1, keepdims=True)).astype(BF16)
        ctx_ref[:, h * HD:(h + 1) * HD] = nt_dot(probs, values).astype(BF16)
    for copy in wo_copies:
        copy.wait()
    leaving = []
    for i in range(8):
        stage[i] = project(ctx_ref, wo_ref, 1 - cc, i)
        leaving.append(leave((stage.at[i], outs[i // 4].at[i % 4]), out_sems, i))
    for i in range(8):
        stage[8 + i] = project(ctx_ref, wo_ref, cc, i)
        leaving.append(leave((stage.at[8 + i], mine_any.at[i]), out_sems, 8 + i))
    for copy in leaving:
        copy.wait()


def leave(blocks, sems, i):
    copy = pltpu.make_async_copy(*blocks, sems.at[i])
    copy.start()
    return copy


def add_body(mine_any, got_a, got_b, out_any, mine_ref, got_ref, stage, sems, out_sems):
    pairs = []
    for i in range(8):
        pairs += [(mine_any.at[i], mine_ref.at[i]), ((got_a, got_b)[i // 4].at[i % 4], got_ref.at[i])]
    copies = fetch(pairs, sems)
    leaving = []
    for i in range(8):
        copies[2 * i].wait()
        copies[2 * i + 1].wait()
        stage[i] = (mine_ref[i].astype(F32) + got_ref[i].astype(F32)).astype(BF16)
        leaving.append(leave((stage.at[i], out_any.at[i]), out_sems, i))
    for copy in leaving:
        copy.wait()


def final_body(got_ref, out_ref):
    total = got_ref[0].astype(F32)
    for i in range(1, 8):
        total += got_ref[i].astype(F32)
    out_ref[...] = total.astype(BF16)


def on_device(hidden, boundaries, wq_old, wk_old, wv_old, wo_old, weights, grads, moment, second):
    bounds = boundaries
    gi = lax.axis_index("grp")
    zl, xx, cc = place()

    zown = send(hidden, zl=1)
    oth = send(hidden, core=1)
    k0 = wk_old.T
    k3, k1 = send(k0, x=1), send(k0, x=-1)

    (parts,) = call(
        first_body, [shape(4, 192, 1024)], weights, grads, moment, second, hidden, oth, bounds,
        in_specs=[HBM] * 6 + [VMEM],
        scratch_shapes=[pltpu.VMEM((64, 4096), BF16)] * 2 + [pltpu.VMEM((64, 4096), F32)] * 2
        + [pltpu.VMEM((TOK, 4096), BF16)] * 2 + [pltpu.SemaphoreType.DMA((8,))],
        cost=4, vmem=60,
    )
    got = swap_all(parts, "tp", X_GROUPS)
    v0 = wv_old.T
    (joined,) = call(
        join_body, [shape(64, WIDE)], after(k3, k1, parts), v0, in_specs=[HBM] * 2, vmem=60, cost=8,
        scratch_shapes=[pltpu.SemaphoreType.DMA((2,))],
    )
    k2v3 = send(joined, x=1)
    v1 = send(after(v0, joined), x=-1)
    got = after(got, joined)
    acc, keep, give = call(
        middle_body, [shape(512, 256)] * 3, got, cost=100,
        in_specs=[ANY],
        scratch_shapes=[pltpu.VMEM((4, 192, 1024), BF16), pltpu.SemaphoreType.DMA((4,))],
    )
    from_zl = send(acc, zl=1)
    got_core = send(give, core=1)

    zoth = send(zown, core=1)
    (shared,) = call(share_body, [shape(4, STEPS, 1024)], acc, from_zl, in_specs=[ANY] * 2,
        scratch_shapes=[pltpu.VMEM((512, 256), BF16)] * 2 + [pltpu.SemaphoreType.DMA((2,))],
    )
    v2 = send(after(v1, shared), x=-1)
    rows_half = swap_all(shared, "tp", X_GROUPS)
    near, far = move([after(keep, shared), got_core], [shape(512, 256)] * 2, cost=0)(spread_pairs, 4)
    far_zl, near_zh, far_zh = send(far, zl=1), send(near, zh=1), send(far, zh=1, zl=1)

    zboth = after((zown, zoth), shared)
    kv = call(
        kv_body, [shape(128, 4 * TOK)] * 4,
        hidden, oth, *zboth, k0, v0, k1, v1, k2v3, v2, k3,
        in_specs=[HBM] * 11,
        scratch_shapes=[
            pltpu.VMEM((256, 4 * TOK), F32), pltpu.VMEM((4, 4 * TOK, 2048), BF16),
            pltpu.VMEM((4, 256, 2048), BF16), pltpu.SemaphoreType.DMA((4, 12)),
        ],
        cost=100, vmem=60,
    )
    kv_parts = [kv[0]] + [send(kv[4 - d], x=-d) for d in (1, 2, 3)]

    (chunks,) = move([near, after(far_zl, *kv), near_zh, far_zh], [shape(2048, 256)], cost=0)(chunk_pairs, 4)
    nears = [send(chunks, y=1), send(chunks, y=3)]
    (kv_mine,) = move([after(kv_parts[0], far_zl, near_zh, far_zh), *kv_parts[1:]], [shape(128, 16 * TOK)])(line_pairs, 4)
    kv_other = send(kv_mine, core=1)
    rows_other = send(rows_half, core=1)
    (token,) = call(token_body, [shape(8, BLOCK, dtype=F32)], rows_other, in_specs=[ANY], cost=100)
    *out_other, mine = call(
        attend_body, [shape(4, STEPS, 512)] * 2 + [shape(8, STEPS, 512)],
        rows_half, rows_other, wq_old, kv_mine, kv_other, bounds, wo_old, token,
        in_specs=[HBM] * 5 + [VMEM, HBM, ANY],
        scratch_shapes=[
            pltpu.VMEM((STEPS, 256), BF16), pltpu.VMEM((128, 16 * TOK), BF16), pltpu.VMEM((128, 16 * TOK), BF16),
            pltpu.VMEM((256, WIDE), BF16), pltpu.VMEM((16, STEPS, 512), BF16),
            pltpu.VMEM((8, STEPS, 1024), BF16), pltpu.VMEM((WIDE, 256), BF16),
            pltpu.SemaphoreType.DMA((2,)), pltpu.SemaphoreType.DMA((16,)), pltpu.SemaphoreType.DMA((16,)),
            pltpu.SemaphoreType.DMA((8,)), pltpu.SemaphoreType.DMA((16,)),
        ],
        out_specs=[ANY] * 3,
        vmem=60,
    )
    out_core = [send(o, core=1) for o in out_other]
    (out,) = call(
        add_body, [shape(8, STEPS, 512)], mine, *out_core, in_specs=[HBM] * 3, out_specs=[ANY], vmem=60,
        scratch_shapes=[pltpu.VMEM((8, STEPS, 512), BF16)] * 3
        + [pltpu.SemaphoreType.DMA((16,)), pltpu.SemaphoreType.DMA((8,))],
    )
    summed = swap_all(out, "tp", ZX_GROUPS)

    spots = [jnp.stack([gi // 4, zl, cc, (gi - d) % 4]).astype(jnp.int32) for d in range(4)]
    nears = after(tuple(nears), out)
    on = move(nears, [shape(1024, 256)] * 2, cost=0)(on_pairs, 2)
    last = [send(on[0], y=1), send(on[1], y=3)]

    def sides(*blocks):
        return [b.reshape(-1, 2, 2, 4, 64, 256) for b in blocks]

    done = quantize(sides(*[after(chunks, out)] * 2), spots[0], ())
    done = quantize(sides(nears[0], nears[0]), spots[1], done)
    done = quantize(sides(nears[1], nears[1]), spots[3], done)
    (step_features,) = call(final_body, [shape(STEPS, 512)], summed)
    last = after(tuple(last), step_features)
    done = quantize(sides(*last), spots[2], done)
    quantized = done[0]
    scales = done[1].T
    return (step_features, quantized, scales)


def solution(mesh):
    placed = (
        P(("grp", "tp"), None),
        P("grp", None),
        P(None, "tp"),
        P(None, "tp"),
        P(None, "tp"),
        P("tp", None),
        P(("grp", "tp"), None),
        P(("grp", "tp"), None),
        P(("grp", "tp"), None),
        P(("grp", "tp"), None),
    )
    return jax.shard_map(
        on_device,
        mesh=mesh,
        in_specs=placed,
        out_specs=(P("grp", "tp"), P(None, "tp"), P(None, "tp")),
        check_vma=False,
    )
```
